32 devices in a mesh: recv: 4 (over z), src: 8 (over y, x, core).
Axes of the slice: x: 2, y: 2, z: 4, core: 2. Of those that a mesh axis runs over, the one named last changes fastest.
Arguments:
- log_rate: float32 [65536], P(('recv', 'src')), may hold values from -2.5 to 2.5
- log_state: float32 [65536], P(('recv', 'src')), may hold values from -1 to 1.5
- a_sigma: float32 [65536], P(('recv', 'src')), may hold values from 1 to 4
- b_sigma: float32 [65536], P(('recv', 'src')), may hold values from 0.5 to 4
- crit_slip: float32 [65536], P(('recv', 'src')), may hold values from 0.5 to 4
- plate_rate: float32 [65536], P(('recv', 'src')), may hold values from 0.25 to 2
- cluster_order: int32 [32, 2048], P(('recv', 'src')), may hold values from 0 to 2047, each once within a row
- near_tiles: bfloat16 [3072, 128, 128], P(('recv', 'src')), may hold values from -1 to 1
- near_pairs: int32 [2, 3072], P(None, 'recv'), may hold values from 0 to 511, as said below
- far_u: bfloat16 [32768, 32, 128], P(('recv', 'src')), may hold values from -0.59765625 to 0.59765625
- far_v: bfloat16 [32768, 32, 128], P(('recv', 'src')), may hold values from -0.59765625 to 0.59765625
- far_pairs: int32 [2, 32768], P(None, ('recv', 'src')), may hold values from 0 to 511, as said below
- far_ranks: int32 [32768], P(('recv', 'src')), may hold values from 8 to 32
Outputs:
- new_log_rate: float32 [65536], P(('recv', 'src'))
- new_log_state: float32 [65536], P(('recv', 'src'))
The draws below stay inside these ranges and needn't reach their ends.
Inputs may be any that keep to these rules, and one draw needn't show every extreme that they name: `cluster_order`: each row is a permutation of 0 to 2047. `near_pairs`: the tiles of device g (positions g * 96 onward) have receiver clusters among g's own clusters g * 16 to g * 16 + 15. The source group of a cluster c is (c // 16) % 8; of one device's tiles at most 24 have sources in one source group, and in every recv row one source group gets exactly 24 tiles from every device of that row. `far_pairs`: the blocks held by the device with recv index a and src index b have receiver clusters owned by devices of recv index a and source clusters in source group b.
All inputs are finite; a program needn't handle non-finite values.
Results may differ from the reference program's by a relative error of at most 0.0035.
Values may be sent and summed in bfloat16 or wider, within the bound.
No kernel may reach another device: no remote copies, remote signals or barrier semaphores. Data moves between devices by JAX's collectives and lax.ppermute only.
A program may use at most 128 MiB of HBM per device.

```python
import math
import jax
import jax.numpy as jnp
from jax import lax

B = 128
RANK = 32
CL_DEV = 16
RGROUPS = 4
CGROUPS = 8
TILE_DEV = 96
FAR_DEV = 1024
CAP = 24
ELEM_DEV = 2048
CLUSTERS = 512
ELEMS = 65536
TILES = 3072
FARS = 32768
DEVICES = 32


def draw_near_pairs(key, part):
    slot_count = CGROUPS * CAP

    def one_device(device_key, row_index, col_index, preferences):
        subkeys = jax.random.split(device_key, 5)
        random_part = jax.random.randint(subkeys[0], (slot_count,), 0, 65536)
        slot_ids = jnp.arange(slot_count, dtype=jnp.int32)
        preference = preferences[slot_ids // CAP]
        scores = jnp.where(preference == 0, 0, random_part + preference * 8192 + 1) * slot_count + slot_ids
        chosen = jnp.argsort(scores, stable=True)[:TILE_DEV]
        chosen = chosen[jax.random.permutation(subkeys[1], TILE_DEV)]
        destination = chosen // CAP
        source_row = jax.random.randint(subkeys[2], (TILE_DEV,), 0, RGROUPS)
        source_part = jax.random.randint(subkeys[3], (TILE_DEV,), 0, CL_DEV)
        target_part = jax.random.randint(subkeys[4], (TILE_DEV,), 0, CL_DEV)
        sources = (source_row * CGROUPS + destination) * CL_DEV + source_part
        targets = (row_index * CGROUPS + col_index) * CL_DEV + target_part
        return (targets.astype(jnp.int32), sources.astype(jnp.int32))

    def one_row(row_key, row_index):
        preferences = jax.random.permutation(jax.random.fold_in(row_key, 7), CGROUPS)
        device_keys = jax.random.split(jax.random.fold_in(row_key, 11), CGROUPS)
        col_ids = jnp.arange(CGROUPS, dtype=jnp.int32)
        return jax.vmap(lambda device_key, col_index: one_device(device_key, row_index, col_index, preferences))(device_keys, col_ids)
    row_keys = jax.random.split(jax.random.fold_in(key, 3), RGROUPS)
    row_ids = jnp.arange(RGROUPS, dtype=jnp.int32)
    targets, sources = jax.vmap(one_row)(row_keys, row_ids)
    return jnp.stack([targets.reshape(-1), sources.reshape(-1)], 0)


def draw_far_pairs(key, part):
    subkeys = jax.random.split(jax.random.fold_in(key, 5), 4)
    shape = (RGROUPS, CGROUPS, FAR_DEV)
    row_ids = jnp.arange(RGROUPS, dtype=jnp.int32)[:, None, None]
    col_ids = jnp.arange(CGROUPS, dtype=jnp.int32)[None, :, None]
    targets = (row_ids * CGROUPS + jax.random.randint(subkeys[0], shape, 0, CGROUPS)) * CL_DEV + jax.random.randint(subkeys[1], shape, 0, CL_DEV)
    sources = (jax.random.randint(subkeys[2], shape, 0, RGROUPS) * CGROUPS + col_ids) * CL_DEV + jax.random.randint(subkeys[3], shape, 0, CL_DEV)
    return jnp.stack([targets.reshape(-1), sources.reshape(-1)], 0).astype(jnp.int32)


def touch_ends(values, own_key, smallest, high):
    longest = values.shape.index(max(values.shape))
    spots = []
    for shift in (0, 1):
        where = [jax.random.randint(jax.random.fold_in(own_key, axis), (), 0, length) for axis, length in enumerate(values.shape)]
        where[longest] = (where[longest] + shift) % values.shape[longest]
        spots.append(tuple(where))
    return values.at[spots[0]].set(smallest).at[spots[1]].set(high)


def block_scale(key, dims, cuts, smallest, largest):
    def one(axis_at, blocks):
        heights = jax.random.uniform(jax.random.fold_in(jax.random.fold_in(key, 6), axis_at), (blocks,), jnp.float32, smallest / len(cuts), largest / len(cuts))
        return jnp.repeat(jnp.exp(heights), dims[axis_at] // blocks).reshape((-1,) + (1,) * (len(dims) - axis_at - 1))

    loudness = one(*cuts[0])
    for cut in cuts[1:]:
        loudness = loudness * one(*cut)
    return loudness


def gaussian(own_key, extent, spread, bound, cuts=(), kind=jnp.bfloat16):
    loudness = block_scale(own_key, extent, cuts, -0.22, 0.18) if cuts else 1.0
    drawn = jax.random.normal(own_key, extent, jnp.float32) * spread * loudness
    return jnp.minimum(jnp.maximum(drawn, -bound), bound).astype(kind)


def setup_inputs(seed: int = 0) -> dict:
    keys = jax.random.split(jax.random.key(seed), 14)
    return {
        "log_rate": gaussian(keys[0], (ELEMS,), 0.5, 2.5, ((0, 32),), jnp.float32),
        "log_state": jnp.clip(-1.0 + 2.5 * jax.random.uniform(keys[1], (ELEMS,), jnp.float32) ** block_scale(keys[1], (ELEMS,), ((0, 32),), -0.2, 0.2), -1.0, 1.5),
        "a_sigma": jnp.clip(jnp.exp(math.log(4.0) - 1.3862944 * jax.random.uniform(keys[2], (ELEMS,), jnp.float32) ** block_scale(keys[2], (ELEMS,), ((0, 32),), -0.2, 0.2)), 1.0, 4.0),
        "b_sigma": jnp.clip(jnp.exp(math.log(4.0) - 2.0794415 * jax.random.uniform(keys[3], (ELEMS,), jnp.float32) ** block_scale(keys[3], (ELEMS,), ((0, 32),), -0.2, 0.2)), 0.5, 4.0),
        "crit_slip": jnp.clip(jnp.exp(math.log(4.0) - 2.0794415 * jax.random.uniform(keys[4], (ELEMS,), jnp.float32) ** block_scale(keys[4], (ELEMS,), ((0, 32),), -0.2, 0.2)), 0.5, 4.0),
        "plate_rate": jnp.clip(jnp.exp(math.log(2.0) - 2.0794415 * jax.random.uniform(keys[5], (ELEMS,), jnp.float32) ** block_scale(keys[5], (ELEMS,), ((0, 32),), -0.2, 0.2)), 0.25, 2.0),
        "cluster_order": jax.vmap(lambda own: jax.random.permutation(own, ELEM_DEV))(jax.random.split(keys[6], DEVICES)).reshape((DEVICES, ELEM_DEV)).astype(jnp.int32),
        "near_tiles": gaussian(keys[7], (TILES, B, B), 0.15, 1.0, ((0, 32),)),
        "near_pairs": draw_near_pairs(jax.random.fold_in(keys[13], 71), 0),
        "far_u": gaussian(keys[9], (FARS, RANK, B), 0.1, 0.59765625, ((0, 32),)),
        "far_v": gaussian(keys[10], (FARS, RANK, B), 0.1, 0.59765625, ((0, 32),)),
        "far_pairs": draw_far_pairs(jax.random.fold_in(keys[13], 71), 0),
        "far_ranks": touch_ends(jax.random.randint(keys[12], (FARS,), RANK // 4, RANK + 1), jax.random.fold_in(keys[12], 1), RANK // 4, RANK).astype(jnp.int32),
    }


time_step = 0.1
damping = 0.5


def stress_rate(deficit, near_tiles, near_pairs, far_u, far_v, far_pairs, far_ranks):
    columns = deficit.reshape(CLUSTERS, B)
    tile_sets = near_tiles.reshape(DEVICES, TILE_DEV, B, B)
    near_source = near_pairs[1].reshape(DEVICES, TILE_DEV)

    def near_piece(pieces):
        tiles, sources = pieces
        rows_in = columns[sources].astype(jnp.float32)
        return jnp.einsum("tij,tj->ti", tiles.astype(jnp.float32), rows_in)

    near_terms = lax.map(near_piece, (tile_sets, near_source))
    total = jnp.zeros((CLUSTERS, B), jnp.float32).at[near_pairs[0]].add(near_terms.reshape(-1, B))
    left_sets = far_u.reshape(DEVICES, FAR_DEV, RANK, B)
    right_sets = far_v.reshape(DEVICES, FAR_DEV, RANK, B)
    far_source = far_pairs[1].reshape(DEVICES, FAR_DEV)
    rank_sets = far_ranks.reshape(DEVICES, FAR_DEV)

    def far_piece(pieces):
        left, right, sources, ranks = pieces
        rows_in = columns[sources].astype(jnp.float32)
        coefficients = jnp.einsum("tkj,tj->tk", right.astype(jnp.float32), rows_in)
        kept = jnp.arange(RANK, dtype=jnp.int32)[None, :] < ranks[:, None]
        coefficients = jnp.where(kept, coefficients, jnp.float32(0.0)).astype(jnp.bfloat16)
        coefficients = lax.optimization_barrier(coefficients).astype(jnp.float32)
        return jnp.einsum("tki,tk->ti", left.astype(jnp.float32), coefficients)

    far_terms = lax.map(far_piece, (left_sets, right_sets, far_source, rank_sets))
    total = total.at[far_pairs[0]].add(far_terms.reshape(-1, B))
    return total.reshape(-1)


def reference(log_rate, log_state, a_sigma, b_sigma, crit_slip, plate_rate, cluster_order, near_tiles, near_pairs, far_u, far_v, far_pairs, far_ranks):
    offsets = (jnp.arange(DEVICES, dtype=jnp.int32) * ELEM_DEV)[:, None]
    positions = (offsets + cluster_order.astype(jnp.int32)).reshape(-1)
    speed_log = log_rate[positions]
    theta_log = log_state[positions]
    a_values = a_sigma[positions]
    b_values = b_sigma[positions]
    slip_scale = crit_slip[positions]
    plate_values = plate_rate[positions]

    def rates(speed_now, theta_now):
        slip_speed = jnp.exp(speed_now)
        deficit = (plate_values - slip_speed).astype(jnp.bfloat16)
        stress = stress_rate(deficit, near_tiles, near_pairs, far_u, far_v, far_pairs, far_ranks)
        theta_rate = jnp.exp(-theta_now) - slip_speed / slip_scale
        speed_rate = (stress - b_values * theta_rate) / (a_values + damping * slip_speed)
        return speed_rate, theta_rate

    first_p, first_q = rates(speed_log, theta_log)
    second_p, second_q = rates(speed_log + time_step * first_p, theta_log + time_step * first_q)
    new_speed = speed_log + 0.5 * time_step * (first_p + second_p)
    new_theta = theta_log + 0.5 * time_step * (first_q + second_q)
    new_log_rate = jnp.zeros((ELEMS,), jnp.float32).at[positions].set(new_speed)
    new_log_state = jnp.zeros((ELEMS,), jnp.float32).at[positions].set(new_theta)
    return new_log_rate, new_log_state
```

```python
import functools

import jax
import jax.numpy as jnp
from jax import lax
from jax.experimental import pallas as pl
from jax.experimental.pallas import tpu as pltpu
from jax.sharding import PartitionSpec as P

time_step = 0.1
damping = 0.5
f32 = jnp.float32
bf16 = jnp.bfloat16
lanes = 128
chunks = 8
vmem_bytes = 40 * 2**20
by_row = (((1,), (1,)), ((), ()))
in_vmem = pl.BlockSpec(memory_space=pltpu.VMEM)
in_smem = pl.BlockSpec(memory_space=pltpu.SMEM)
anywhere = pl.BlockSpec(memory_space=pl.ANY)


def order_kernel(p_ref, q_ref, a_ref, b_ref, slip_ref, plate_ref, order_ref, own_ref, shared_ref, deficit_ref):
    order = order_ref[...]
    row, lane = order // lanes, order % lanes
    rows = order.shape[0]
    refs = (p_ref, q_ref, a_ref, b_ref, slip_ref, plate_ref)
    sorted_values = [jnp.zeros(order.shape, f32)] * len(refs)
    for r in range(rows):
        here = row == r
        for k, ref in enumerate(refs):
            spread = jnp.broadcast_to(ref[r : r + 1, :], order.shape)
            got = jnp.take_along_axis(spread, lane, axis=1)
            sorted_values[k] = jnp.where(here, got, sorted_values[k])
    p, q, a, b, slip, plate = sorted_values
    speed = jnp.exp(p)
    theta_rate = jnp.exp(-q) - speed / slip
    gain = 1.0 / (a + damping * speed)
    for k, value in enumerate((p, q, a, b, slip, plate, theta_rate, gain)):
        own_ref[k] = value
    shared_ref[0] = p - time_step * b * theta_rate * gain
    shared_ref[1] = time_step * gain
    shared_ref[2] = plate
    deficit_ref[...] = (plate - speed).astype(bf16)


def table_kernel(source_ref, target_ref, rank_ref, source_out, target_out, *, rank):
    per_row = lanes // rank
    group = lanes // per_row
    shape = (group, lanes)
    lane = lax.broadcasted_iota(jnp.int32, shape, 1)
    pick = lax.broadcasted_iota(jnp.int32, shape, 0) * per_row + lane // rank
    for a in range(source_ref.shape[0]):
        def spread(ref):
            return jnp.take_along_axis(jnp.broadcast_to(ref[a : a + 1, :], shape), pick, axis=1)

        where = slice(a * group, (a + 1) * group)
        source_out[where, :] = jnp.where(lane % rank < spread(rank_ref), spread(source_ref), -1)
        target_out[where, :] = spread(target_ref).astype(f32)


def far_part(source_ref, target_ref, deficit_ref, v_buf, u_buf, out_ref, before):
    factor_rows = v_buf.shape[0]
    part = factor_rows // chunks
    source_count = deficit_ref.shape[0]
    target_count = out_ref.shape[0]
    deficit = deficit_ref[...]
    source_ids = lax.broadcasted_iota(jnp.int32, (source_count, lanes), 0)
    target_ids = [
        (lax.broadcasted_iota(jnp.int32, (16, lanes), 0) + 16 * k).astype(f32).astype(bf16)
        for k in range(target_count // 16)
    ]
    out_ref[...] = jnp.zeros_like(out_ref)

    def step(i, _):
        before(i)
        base = pl.multiple_of(i * part, part)
        products = lax.dot_general(
            deficit, v_buf[pl.ds(base, part), :], by_row, preferred_element_type=f32
        )
        spread = []
        for k in range(part // lanes):
            row = i * (part // lanes) + k
            source = source_ref[pl.ds(row, 1), :]
            target = jnp.broadcast_to(target_ref[pl.ds(row, 1), :], (16, lanes)).astype(bf16)
            coef = jnp.sum(
                jnp.where(source_ids == source, products[:, k * lanes : (k + 1) * lanes], 0.0),
                axis=0,
                keepdims=True,
            )
            coef = jnp.broadcast_to(coef, (16, lanes)).astype(bf16)
            spread.append(
                jnp.concatenate(
                    [jnp.where(ids == target, coef, jnp.zeros_like(coef)) for ids in target_ids], 0
                )
            )
        out_ref[...] += jnp.dot(
            jnp.concatenate(spread, 1), u_buf[pl.ds(base, part), :], preferred_element_type=f32
        )
        return 0

    lax.fori_loop(0, chunks, step, 0)


def near_part(source_ref, target_ref, columns_ref, tile_buf, columns_buf, count):
    tile_count = tile_buf.shape[0]
    columns_buf[...] = columns_ref[...].astype(f32)
    ids = lax.broadcasted_iota(jnp.int32, (count, lanes), 0)
    total = jnp.zeros((count, lanes), f32)
    for t in range(tile_count):
        deficit = jnp.broadcast_to(columns_buf[pl.ds(source_ref[t], 1), :], (count, lanes))
        placed = jnp.where(ids == target_ref[t], deficit, 0.0).astype(bf16)
        total += lax.dot_general(placed, tile_buf[t], by_row, preferred_element_type=f32)
    return total


def far_copies(v_hbm, u_hbm, v_buf, u_buf, sems):
    part = v_hbm.shape[0] // chunks

    def copies(i):
        where = pl.ds(pl.multiple_of(i * part, part), part)
        return (
            pltpu.make_async_copy(v_hbm.at[where], v_buf.at[where], sems.at[0, i]),
            pltpu.make_async_copy(u_hbm.at[where], u_buf.at[where], sems.at[1, i]),
        )

    return copies


def both_kernel(
    near_source, near_target, own_row, source_ref, target_ref, deficit_ref, columns_ref, v_hbm, u_hbm, tiles_hbm,
    out_ref, v_buf, u_buf, tile_buf, columns_buf, total_ref, sems, tile_sem,
):
    copies = far_copies(v_hbm, u_hbm, v_buf, u_buf, sems)
    for i in range(chunks):
        for copy in copies(i):
            copy.start()
    tile_copy = pltpu.make_async_copy(tiles_hbm, tile_buf, tile_sem)
    tile_copy.start()

    def before(i):
        for copy in copies(i):
            copy.wait()

    far_part(source_ref, target_ref, deficit_ref, v_buf, u_buf, total_ref, before)
    tile_copy.wait()
    count = out_ref.shape[1]
    near = near_part(near_source, near_target, columns_ref, tile_buf, columns_buf, count)
    own = pl.ds(pl.multiple_of(own_row[0] * count, count), count)
    total_ref[own, :] += near
    out_ref[...] = jnp.broadcast_to(
        total_ref[...].astype(bf16).reshape(1, -1, count, lanes), (out_ref.shape[0] // (total_ref.shape[0] // count), total_ref.shape[0] // count, count, lanes)
    ).reshape(out_ref.shape)


def far_kernel(
    source_ref, target_ref, deficit_ref, v_hbm, u_hbm, out_ref, v_buf, u_buf, total_ref, sems
):
    copies = far_copies(v_hbm, u_hbm, v_buf, u_buf, sems)
    for i in range(chunks):
        for copy in copies(i):
            copy.start()

    def before(i):
        for copy in copies(i):
            copy.wait()

    far_part(source_ref, target_ref, deficit_ref, v_buf, u_buf, total_ref, before)
    out_ref[...] = total_ref[...].astype(bf16)


def near_kernel(near_source, near_target, columns_ref, tile_buf, out_ref, columns_buf):
    out_ref[...] = near_part(
        near_source, near_target, columns_ref, tile_buf, columns_buf, out_ref.shape[0]
    )


def final_kernel(own_ref, first_ref, second_ref, near_ref, order_ref, p_out, q_out):
    p, q, a, b, slip, plate, theta_rate, gain = [own_ref[k] for k in range(8)]
    first_p = (first_ref[...] - b * theta_rate) * gain
    speed = jnp.exp(p + time_step * first_p)
    second_q = jnp.exp(-(q + time_step * theta_rate)) - speed / slip
    stress = jnp.sum(second_ref[...].astype(f32), axis=0) + near_ref[...]
    second_p = (stress - b * second_q) / (a + damping * speed)
    new_p = p + 0.5 * time_step * (first_p + second_p)
    new_q = q + 0.5 * time_step * (theta_rate + second_q)
    pieces = []
    for value in (new_p, new_q):
        for _ in range(3):
            piece = value.astype(bf16).astype(f32)
            value = value - piece
            pieces.append(piece)
    rows = p.shape[0]
    order = order_ref[...]
    row, lane = order // lanes, order % lanes
    row_ids = lax.broadcasted_iota(jnp.int32, (rows, lanes), 0)
    lane_ids = lax.broadcasted_iota(jnp.int32, (lanes, lanes), 0)
    total = jnp.zeros((len(pieces) * rows, lanes), f32)
    for r in range(rows):
        here = row_ids == row[r : r + 1, :]
        placed = jnp.concatenate(
            [jnp.where(here, piece[r : r + 1, :], 0.0) for piece in pieces], 0
        ).astype(bf16)
        spread = jnp.where(lane_ids == lane[r : r + 1, :], 1.0, 0.0).astype(bf16)
        total += lax.dot_general(placed, spread, by_row, preferred_element_type=f32)
    for k, out in enumerate((p_out, q_out)):
        high, mid, low = [total[(3 * k + j) * rows : (3 * k + j + 1) * rows, :] for j in range(3)]
        out[...] = (low + mid) + high


def on_device(
    log_rate,
    log_state,
    a_sigma,
    b_sigma,
    crit_slip,
    plate_rate,
    cluster_order,
    near_tiles,
    near_pairs,
    far_u,
    far_v,
    far_pairs,
    far_ranks,
):
    src_count = lax.axis_size("src")
    recv_count = lax.axis_size("recv")
    device_count = src_count * recv_count
    recv_index = lax.axis_index("recv")
    src_index = lax.axis_index("src")
    tile_count = near_tiles.shape[0]
    own_clusters = log_rate.shape[0] // lanes
    group_rows = own_clusters * src_count
    source_rows = own_clusters * recv_count
    far_count, rank = far_u.shape[:2]
    factor_rows = far_count * rank
    params = pltpu.CompilerParams(vmem_limit_bytes=vmem_bytes)
    whole = (own_clusters, lanes)

    order = cluster_order.reshape(whole)
    own, shared, deficit = pl.pallas_call(
        order_kernel,
        out_shape=(
            jax.ShapeDtypeStruct((8,) + whole, f32),
            jax.ShapeDtypeStruct((3,) + whole, f32),
            jax.ShapeDtypeStruct(whole, bf16),
        ),
    )(*[x.reshape(whole) for x in (log_rate, log_state, a_sigma, b_sigma, crit_slip, plate_rate)], order)

    columns = lax.all_to_all(
        jnp.broadcast_to(deficit[None], (device_count,) + whole),
        ("recv", "src"), split_axis=0, concat_axis=0, tiled=True,
    )
    shared_columns = lax.all_gather(shared, "recv", axis=1, tiled=True)

    near_own = lax.dynamic_slice_in_dim(near_pairs, src_index * tile_count, tile_count, 1)
    near_target = near_own[0] - (recv_index * group_rows + src_index * own_clusters)
    near_source = near_own[1]
    far_target = far_pairs[0] - recv_index * group_rows
    far_source = far_pairs[1] // group_rows * own_clusters + far_pairs[1] % own_clusters
    table = (factor_rows // lanes, lanes)
    source_table, target_table = pl.pallas_call(
        functools.partial(table_kernel, rank=rank),
        out_shape=(jax.ShapeDtypeStruct(table, jnp.int32), jax.ShapeDtypeStruct(table, f32)),
    )(*[x.reshape(far_count // lanes, lanes) for x in (far_source, far_target, far_ranks)])

    v_rows = far_v.reshape(factor_rows, lanes)
    u_rows = far_u.reshape(factor_rows, lanes)
    far_scratch = [
        pltpu.VMEM(v_rows.shape, bf16),
        pltpu.VMEM(u_rows.shape, bf16),
    ]
    total_scratch = pltpu.VMEM((group_rows, lanes), f32)
    columns_scratch = pltpu.VMEM((own_clusters * device_count, lanes), f32)
    far_sems = pltpu.SemaphoreType.DMA((2, chunks))

    group_columns = lax.dynamic_index_in_dim(
        columns.reshape((recv_count, src_count) + whole), src_index, 1, keepdims=False
    ).reshape(source_rows, lanes)
    partial = pl.pallas_call(
        both_kernel,
        in_specs=[in_smem] * 3 + [in_vmem] * 4 + [anywhere] * 3,
        out_specs=in_vmem,
        out_shape=jax.ShapeDtypeStruct((device_count,) + whole, bf16),
        scratch_shapes=far_scratch
        + [pltpu.VMEM(near_tiles.shape, bf16), columns_scratch, total_scratch, far_sems, pltpu.SemaphoreType.DMA],
        compiler_params=params,
    )(
        near_source, near_target, src_index.reshape(1), source_table, target_table,
        group_columns, columns.reshape(-1, lanes), v_rows, u_rows, near_tiles,
    )
    stress_parts = lax.all_to_all(
        partial, ("recv", "src"), split_axis=0, concat_axis=0, tiled=True
    )
    first_stress = jnp.sum(
        stress_parts.reshape((recv_count, src_count) + whole).astype(f32), axis=1
    )
    second_deficit = (
        shared_columns[2]
        - jnp.exp(shared_columns[0] + shared_columns[1] * first_stress.reshape(-1, lanes))
    ).astype(bf16)
    own_stress = lax.dynamic_index_in_dim(first_stress, recv_index, 0, keepdims=False)

    by_group = lax.all_gather(second_deficit.reshape((1, recv_count) + whole), "src", axis=0, tiled=True)
    second_columns = by_group.transpose(1, 0, 2, 3).reshape(-1, lanes)
    far_second = pl.pallas_call(
        far_kernel,
        in_specs=[in_vmem] * 3 + [anywhere] * 2,
        out_specs=in_vmem,
        out_shape=jax.ShapeDtypeStruct((group_rows, lanes), bf16),
        scratch_shapes=far_scratch + [total_scratch, far_sems],
        compiler_params=params,
    )(source_table, target_table, second_deficit, v_rows, u_rows)
    second_parts = lax.all_to_all(far_second, "src", split_axis=0, concat_axis=0, tiled=True)
    near_second = pl.pallas_call(
        near_kernel,
        in_specs=[in_smem] * 2 + [in_vmem] * 2,
        out_specs=in_vmem,
        out_shape=jax.ShapeDtypeStruct(whole, f32),
        scratch_shapes=[columns_scratch],
        compiler_params=params,
    )(near_source, near_target, second_columns, near_tiles)
    new_p, new_q = pl.pallas_call(
        final_kernel,
        out_shape=(jax.ShapeDtypeStruct(whole, f32), jax.ShapeDtypeStruct(whole, f32)),
    )(own, own_stress, second_parts.reshape((src_count,) + whole), near_second, order)
    return new_p.reshape(-1), new_q.reshape(-1)


def solution(mesh):
    return jax.shard_map(
        on_device,
        mesh=mesh,
        in_specs=(
            P(("recv", "src")),
            P(("recv", "src")),
            P(("recv", "src")),
            P(("recv", "src")),
            P(("recv", "src")),
            P(("recv", "src")),
            P(("recv", "src"), None),
            P(("recv", "src"), None, None),
            P(None, "recv"),
            P(("recv", "src"), None, None),
            P(("recv", "src"), None, None),
            P(None, ("recv", "src")),
            P(("recv", "src")),
        ),
        out_specs=(P(("recv", "src")), P(("recv", "src"))),
        check_vma=False,
    )
```

```python
import functools

import jax
import jax.numpy as jnp
from jax import lax
from jax.experimental import pallas as pl
from jax.experimental.pallas import tpu as pltpu
from jax.sharding import PartitionSpec as P

time_step = 0.1
damping = 0.5
f32 = jnp.float32
bf16 = jnp.bfloat16
lanes = 128
chunks = 8
vmem_bytes = 8 * 2**20
far_vmem_bytes = 58 * 2**20
by_row = (((1,), (1,)), ((), ()))
in_vmem = pl.BlockSpec(memory_space=pltpu.VMEM)
in_hbm = pl.BlockSpec(memory_space=pl.ANY)
in_smem = pl.BlockSpec(memory_space=pltpu.SMEM)


def order_kernel(p_ref, q_ref, a_ref, b_ref, slip_ref, plate_ref, order_ref, own_ref, shared_ref):
    order = order_ref[...]
    row, lane = order // lanes, order % lanes
    rows = order.shape[0]
    refs = (p_ref, q_ref, a_ref, b_ref, slip_ref, plate_ref)
    sorted_values = [jnp.zeros(order.shape, f32)] * len(refs)
    for r in range(rows):
        here = row == r
        for k, ref in enumerate(refs):
            spread = jnp.broadcast_to(ref[r : r + 1, :], order.shape)
            got = jnp.take_along_axis(spread, lane, axis=1)
            sorted_values[k] = jnp.where(here, got, sorted_values[k])
    p, q, a, b, slip, plate = sorted_values
    speed = jnp.exp(p)
    theta_rate = jnp.exp(-q) - speed / slip
    gain = 1.0 / (a + damping * speed)
    for k, value in enumerate((p, q, a, b, slip, plate, theta_rate, gain)):
        own_ref[k] = value
    shared_ref[0] = p - time_step * b * theta_rate * gain
    shared_ref[1] = time_step * gain
    shared_ref[2] = plate
    shared_ref[3] = (plate - speed).astype(bf16).astype(f32)


def table_kernel(source_ref, target_ref, rank_ref, source_out, target_out, *, rank):
    per_row = lanes // rank
    group = lanes // per_row
    shape = (group, lanes)
    lane = lax.broadcasted_iota(jnp.int32, shape, 1)
    pick = lax.broadcasted_iota(jnp.int32, shape, 0) * per_row + lane // rank
    for a in range(source_ref.shape[0]):
        def spread(ref):
            return jnp.take_along_axis(jnp.broadcast_to(ref[a : a + 1, :], shape), pick, axis=1)

        where = slice(a * group, (a + 1) * group)
        source_out[where, :] = jnp.where(lane % rank < spread(rank_ref), spread(source_ref), -1)
        target_out[where, :] = spread(target_ref).astype(f32)


def far_part(source_ref, target_ref, deficit_ref, v_buf, u_buf, out_ref, before):
    factor_rows = v_buf.shape[0]
    part = factor_rows // chunks
    source_count = deficit_ref.shape[0]
    target_count = out_ref.shape[0]
    deficit = deficit_ref[...]
    source_ids = lax.broadcasted_iota(jnp.int32, (source_count, lanes), 0)
    target_ids = [
        (lax.broadcasted_iota(jnp.int32, (16, lanes), 0) + 16 * k).astype(f32).astype(bf16)
        for k in range(target_count // 16)
    ]
    out_ref[...] = jnp.zeros_like(out_ref)

    def step(i, _):
        before(i)
        base = pl.multiple_of(i * part, part)
        products = lax.dot_general(
            deficit, v_buf[pl.ds(base, part), :], by_row, preferred_element_type=f32
        )
        spread = []
        for k in range(part // lanes):
            row = i * (part // lanes) + k
            source = source_ref[pl.ds(row, 1), :]
            target = jnp.broadcast_to(target_ref[pl.ds(row, 1), :], (16, lanes)).astype(bf16)
            coef = jnp.sum(
                jnp.where(source_ids == source, products[:, k * lanes : (k + 1) * lanes], 0.0),
                axis=0,
                keepdims=True,
            )
            coef = jnp.broadcast_to(coef, (16, lanes)).astype(bf16)
            spread.append(
                jnp.concatenate(
                    [jnp.where(ids == target, coef, jnp.zeros_like(coef)) for ids in target_ids], 0
                )
            )
        out_ref[...] += jnp.dot(
            jnp.concatenate(spread, 1), u_buf[pl.ds(base, part), :], preferred_element_type=f32
        )
        return 0

    lax.fori_loop(0, chunks, step, 0)


def near_part(source_ref, target_ref, columns_ref, tile_buf, columns_buf, count):
    tile_count = tile_buf.shape[0]
    columns_buf[...] = columns_ref[...].astype(f32)
    ids = lax.broadcasted_iota(jnp.int32, (count, lanes), 0)
    total = jnp.zeros((count, lanes), f32)
    for t in range(tile_count):
        deficit = jnp.broadcast_to(columns_buf[pl.ds(source_ref[t], 1), :], (count, lanes))
        placed = jnp.where(ids == target_ref[t], deficit, 0.0).astype(bf16)
        total += lax.dot_general(placed, tile_buf[t], by_row, preferred_element_type=f32)
    return total


def far_stream(source_ref, target_ref, deficit_ref, v_hbm, u_hbm, out_ref, v_buf, u_buf, sems):
    part = v_hbm.shape[0] // chunks

    def copies(i):
        where = pl.ds(pl.multiple_of(i * part, part), part)
        return (
            pltpu.make_async_copy(v_hbm.at[where], v_buf.at[where], sems.at[0, i]),
            pltpu.make_async_copy(u_hbm.at[where], u_buf.at[where], sems.at[1, i]),
        )

    for i in range(chunks):
        for copy in copies(i):
            copy.start()

    def before(i):
        for copy in copies(i):
            copy.wait()

    far_part(source_ref, target_ref, deficit_ref, v_buf, u_buf, out_ref, before)


def far_kernel(source_ref, target_ref, deficit_ref, v_hbm, u_hbm, out_ref, v_buf, u_buf, sems):
    far_stream(source_ref, target_ref, deficit_ref, v_hbm, u_hbm, out_ref, v_buf, u_buf, sems)


def far_send_kernel(
    source_ref, target_ref, deficit_ref, v_hbm, u_hbm, out_ref, v_buf, u_buf, sems, total_ref
):
    far_stream(source_ref, target_ref, deficit_ref, v_hbm, u_hbm, total_ref, v_buf, u_buf, sems)
    out_ref[...] = total_ref[...].astype(bf16)


def near_kernel(near_source, near_target, columns_ref, tile_ref, out_ref, columns_buf):
    out_ref[...] = near_part(
        near_source, near_target, columns_ref, tile_ref, columns_buf, out_ref.shape[0]
    )


def near_send_kernel(
    near_source, near_target, own_row, far_ref, columns_ref, tile_ref, out_ref, columns_buf, total_ref
):
    count = out_ref.shape[1]
    near = near_part(near_source, near_target, columns_ref, tile_ref, columns_buf, count)
    total_ref[...] = far_ref[...]
    own = pl.ds(pl.multiple_of(own_row[0] * count, count), count)
    total_ref[own, :] += near
    total = total_ref[...].astype(bf16).reshape(-1, count, lanes)
    groups = total.shape[0]
    for k in range(out_ref.shape[0] // groups):
        out_ref[k * groups : (k + 1) * groups] = total


def join_kernel(*refs):
    parts, (columns_ref, send_ref) = refs[:-2], refs[-2:]
    columns = jnp.concatenate([part[3] for part in parts], 0).astype(bf16)
    columns_ref[...] = columns
    for k in range(send_ref.shape[0]):
        send_ref[k] = columns


def update_kernel(recv_ref, stress_ref, *refs):
    parts, (columns_ref, send_ref, own_ref) = refs[:-3], refs[-3:]
    group = stress_ref.shape[0] // len(parts)
    columns = []
    for k, part in enumerate(parts):
        first = (recv_ref[0] ^ k) * group
        stress = stress_ref[first].astype(f32)
        for b in range(1, group):
            stress += stress_ref[first + b].astype(f32)
        if k == 0:
            own_ref[...] = stress
        columns.append(part[2] - jnp.exp(part[0] + part[1] * stress))
    columns = jnp.concatenate(columns, 0).astype(bf16)
    columns_ref[...] = columns
    for k in range(send_ref.shape[0]):
        send_ref[k] = columns


def final_kernel(own_ref, first_ref, second_ref, near_ref, order_ref, p_out, q_out):
    p, q, a, b, slip, plate, theta_rate, gain = [own_ref[k] for k in range(8)]
    first_p = (first_ref[...] - b * theta_rate) * gain
    speed = jnp.exp(p + time_step * first_p)
    second_q = jnp.exp(-(q + time_step * theta_rate)) - speed / slip
    stress = jnp.sum(second_ref[...].astype(f32), axis=0) + near_ref[...]
    second_p = (stress - b * second_q) / (a + damping * speed)
    new_p = p + 0.5 * time_step * (first_p + second_p)
    new_q = q + 0.5 * time_step * (theta_rate + second_q)
    pieces = []
    for value in (new_p, new_q):
        for _ in range(3):
            piece = value.astype(bf16).astype(f32)
            value = value - piece
            pieces.append(piece)
    rows = p.shape[0]
    order = order_ref[...]
    row, lane = order // lanes, order % lanes
    row_ids = lax.broadcasted_iota(jnp.int32, (rows, lanes), 0)
    lane_ids = lax.broadcasted_iota(jnp.int32, (lanes, lanes), 0)
    total = jnp.zeros((len(pieces) * rows, lanes), f32)
    for r in range(rows):
        here = row_ids == row[r : r + 1, :]
        placed = jnp.concatenate(
            [jnp.where(here, piece[r : r + 1, :], 0.0) for piece in pieces], 0
        ).astype(bf16)
        spread = jnp.where(lane_ids == lane[r : r + 1, :], 1.0, 0.0).astype(bf16)
        total += lax.dot_general(placed, spread, by_row, preferred_element_type=f32)
    for k, out in enumerate((p_out, q_out)):
        high, mid, low = [total[(3 * k + j) * rows : (3 * k + j + 1) * rows, :] for j in range(3)]
        out[...] = (low + mid) + high


def on_device(
    log_rate,
    log_state,
    a_sigma,
    b_sigma,
    crit_slip,
    plate_rate,
    cluster_order,
    near_tiles,
    near_pairs,
    far_u,
    far_v,
    far_pairs,
    far_ranks,
):
    src_count = lax.axis_size("src")
    recv_count = lax.axis_size("recv")
    device_count = src_count * recv_count
    recv_index = lax.axis_index("recv")
    src_index = lax.axis_index("src")
    tile_count = near_tiles.shape[0]
    own_clusters = log_rate.shape[0] // lanes
    group_rows = own_clusters * src_count
    source_rows = own_clusters * recv_count
    far_count, rank = far_u.shape[:2]
    factor_rows = far_count * rank
    params = pltpu.CompilerParams(vmem_limit_bytes=vmem_bytes)
    whole = (own_clusters, lanes)

    order = cluster_order.reshape(whole)
    own, shared = pl.pallas_call(
        order_kernel,
        out_shape=(
            jax.ShapeDtypeStruct((8,) + whole, f32),
            jax.ShapeDtypeStruct((4,) + whole, f32),
        ),
        compiler_params=params,
    )(*[x.reshape(whole) for x in (log_rate, log_state, a_sigma, b_sigma, crit_slip, plate_rate)], order)

    parts = [shared] + [
        lax.ppermute(shared, "recv", [(i, i ^ k) for i in range(recv_count)])
        for k in range(1, recv_count)
    ]
    columns_shape = jax.ShapeDtypeStruct((source_rows, lanes), bf16)
    send_shape = jax.ShapeDtypeStruct((src_count, source_rows, lanes), bf16)
    first_columns, first_send = pl.pallas_call(
        join_kernel, out_shape=(columns_shape, send_shape), compiler_params=params
    )(*parts)
    all_first = lax.all_to_all(first_send, "src", split_axis=0, concat_axis=0, tiled=True)

    near_own = lax.dynamic_slice_in_dim(near_pairs, src_index * tile_count, tile_count, 1)
    near_target = near_own[0] - (recv_index * group_rows + src_index * own_clusters)

    def group_place(cluster):
        return ((cluster // group_rows) ^ recv_index) * own_clusters + cluster % own_clusters

    near_source = near_own[1] // own_clusters % src_count * source_rows + group_place(near_own[1])
    far_target = far_pairs[0] - recv_index * group_rows
    far_source = group_place(far_pairs[1])
    table = (factor_rows // lanes, lanes)
    source_table, target_table = pl.pallas_call(
        functools.partial(table_kernel, rank=rank),
        out_shape=(jax.ShapeDtypeStruct(table, jnp.int32), jax.ShapeDtypeStruct(table, f32)),
        compiler_params=params,
    )(*[x.reshape(far_count // lanes, lanes) for x in (far_source, far_target, far_ranks)])

    v_rows = far_v.reshape(factor_rows, lanes)
    u_rows = far_u.reshape(factor_rows, lanes)
    far_specs = dict(
        in_specs=[in_vmem] * 3 + [in_hbm] * 2,
        out_specs=in_vmem,
        compiler_params=pltpu.CompilerParams(vmem_limit_bytes=far_vmem_bytes),
        cost_estimate=pl.CostEstimate(
            flops=2 * factor_rows * lanes * (source_rows + group_rows), bytes_accessed=2**24, transcendentals=0
        ),
    )
    far_scratch = [
        pltpu.VMEM(v_rows.shape, bf16),
        pltpu.VMEM(u_rows.shape, bf16),
        pltpu.SemaphoreType.DMA((2, chunks)),
    ]
    columns_scratch = pltpu.VMEM((own_clusters * device_count, lanes), f32)
    total_scratch = pltpu.VMEM((group_rows, lanes), f32)

    first_far = pl.pallas_call(
        far_kernel,
        out_shape=jax.ShapeDtypeStruct((group_rows, lanes), f32),
        scratch_shapes=far_scratch,
        **far_specs,
    )(source_table, target_table, first_columns, v_rows, u_rows)
    partial = pl.pallas_call(
        near_send_kernel,
        in_specs=[in_smem] * 3 + [in_vmem] * 3,
        out_specs=in_vmem,
        out_shape=jax.ShapeDtypeStruct((device_count,) + whole, bf16),
        scratch_shapes=[columns_scratch, total_scratch],
        compiler_params=params,
    )(near_source, near_target, src_index.reshape(1), first_far, all_first.reshape(-1, lanes), near_tiles)
    stress_parts = lax.all_to_all(partial, ("recv", "src"), split_axis=0, concat_axis=0, tiled=True)

    second_columns, second_send, first_stress = pl.pallas_call(
        update_kernel,
        in_specs=[in_smem] + [in_vmem] * (1 + recv_count),
        out_specs=(in_vmem, in_vmem, in_vmem),
        out_shape=(columns_shape, send_shape, jax.ShapeDtypeStruct(whole, f32)),
        compiler_params=params,
    )(recv_index.reshape(1), stress_parts, *parts)
    all_second = lax.all_to_all(second_send, "src", split_axis=0, concat_axis=0, tiled=True)
    second_far = pl.pallas_call(
        far_send_kernel,
        out_shape=jax.ShapeDtypeStruct((group_rows, lanes), bf16),
        scratch_shapes=far_scratch + [total_scratch],
        **far_specs,
    )(source_table, target_table, second_columns, v_rows, u_rows)
    second_parts = lax.all_to_all(
        second_far.reshape((src_count,) + whole), "src", split_axis=0, concat_axis=0, tiled=True
    )
    second_near = pl.pallas_call(
        near_kernel,
        in_specs=[in_smem] * 2 + [in_vmem] * 2,
        out_specs=in_vmem,
        out_shape=jax.ShapeDtypeStruct(whole, f32),
        scratch_shapes=[columns_scratch],
        compiler_params=params,
    )(near_source, near_target, all_second.reshape(-1, lanes), near_tiles)
    new_p, new_q = pl.pallas_call(
        final_kernel,
        out_shape=(jax.ShapeDtypeStruct(whole, f32), jax.ShapeDtypeStruct(whole, f32)),
        compiler_params=params,
    )(own, first_stress, second_parts, second_near, order)
    return new_p.reshape(-1), new_q.reshape(-1)


def solution(mesh):
    return jax.shard_map(
        on_device,
        mesh=mesh,
        in_specs=(
            P(("recv", "src")),
            P(("recv", "src")),
            P(("recv", "src")),
            P(("recv", "src")),
            P(("recv", "src")),
            P(("recv", "src")),
            P(("recv", "src"), None),
            P(("recv", "src"), None, None),
            P(None, "recv"),
            P(("recv", "src"), None, None),
            P(("recv", "src"), None, None),
            P(None, ("recv", "src")),
            P(("recv", "src")),
        ),
        out_specs=(P(("recv", "src")), P(("recv", "src"))),
        check_vma=False,
    )
```

```python
import functools

import jax
import jax.numpy as jnp
from jax import lax
from jax.experimental import pallas as pl
from jax.experimental.pallas import tpu as pltpu
from jax.sharding import PartitionSpec as P

time_step = 0.1
damping = 0.5
f32 = jnp.float32
bf16 = jnp.bfloat16
lanes = 128
chunks = 8
near_chunks = 4
vmem_bytes = 8 * 2**20
far_vmem_bytes = 28 * 2**20
bodies = (1, 2, 2, 2, 1)
by_row = (((1,), (1,)), ((), ()))
in_vmem = pl.BlockSpec(memory_space=pltpu.VMEM)
anywhere = pl.BlockSpec(memory_space=pl.ANY)
in_smem = pl.BlockSpec(memory_space=pltpu.SMEM)


def in_hbm(x):
    return pltpu.with_memory_space_constraint(x, pltpu.HBM)


def order_kernel(*refs):
    arguments, (own_ref, shared_ref, order_out, buf, order_buf, sems) = refs[:7], refs[7:]
    count = len(arguments) - 1
    copies = [
        pltpu.make_async_copy(ref, order_buf if k == count else buf.at[k], sems.at[k])
        for k, ref in enumerate(arguments)
    ]
    for copy in copies:
        copy.start()
    for copy in copies:
        copy.wait()
    order = order_buf[...]
    order_out[...] = order
    row, lane = order // lanes, order % lanes
    rows = order.shape[0]
    sorted_values = [jnp.zeros(order.shape, f32)] * count
    for r in range(rows):
        here = row == r
        for k in range(count):
            spread = jnp.broadcast_to(buf[k, r : r + 1, :], order.shape)
            got = jnp.take_along_axis(spread, lane, axis=1)
            sorted_values[k] = jnp.where(here, got, sorted_values[k])
    p, q, a, b, slip, plate = sorted_values
    speed = jnp.exp(p)
    theta_rate = jnp.exp(-q) - speed / slip
    gain = 1.0 / (a + damping * speed)
    for k, value in enumerate((p, q, a, b, slip, plate, theta_rate, gain)):
        own_ref[k] = value
    shared_ref[0] = p - time_step * b * theta_rate * gain
    shared_ref[1] = time_step * gain
    shared_ref[2] = plate
    shared_ref[3] = (plate - speed).astype(bf16).astype(f32)


def table_kernel(
    near_pairs, far_pairs_hbm, rank_hbm, source_out, target_out, near_hot_out, near_target_out,
    far_pairs, rank_ref, hot_buf, sems, *, rank, own_clusters, src_count,
):
    copies = (
        pltpu.make_async_copy(far_pairs_hbm, far_pairs, sems.at[0]),
        pltpu.make_async_copy(rank_hbm, rank_ref, sems.at[1]),
    )
    for copy in copies:
        copy.start()
    recv_index, src_index = lax.axis_index("recv"), lax.axis_index("src")
    group_rows = own_clusters * src_count
    source_rows = own_clusters * lax.axis_size("recv")

    def group_place(cluster):
        return ((cluster // group_rows) ^ recv_index) * own_clusters + cluster % own_clusters

    tile_count, cluster_count = hot_buf.shape
    cluster_ids = lax.broadcasted_iota(jnp.int32, (1, cluster_count), 1)
    first_own = recv_index * group_rows + src_index * own_clusters
    for t in range(tile_count):
        source = near_pairs[1, src_index * tile_count + t]
        place = (source // own_clusters) % src_count * source_rows + group_place(source)
        hot_buf[t : t + 1, :] = jnp.where(cluster_ids == place, 1.0, 0.0)
        near_target_out[t : t + 1, :] = jnp.full(
            (1, lanes), near_pairs[0, src_index * tile_count + t] - first_own, jnp.int32
        )
    near_hot_out[...] = hot_buf[...].astype(bf16)

    for copy in copies:
        copy.wait()
    per_row = lanes // rank
    group = lanes // per_row
    shape = (group, lanes)
    lane = lax.broadcasted_iota(jnp.int32, shape, 1)
    pick = lax.broadcasted_iota(jnp.int32, shape, 0) * per_row + lane // rank

    def spread(row):
        return jnp.take_along_axis(jnp.broadcast_to(row, shape), pick, axis=1)

    for a in range(rank_ref.shape[0]):
        where = slice(a * group, (a + 1) * group)
        across = slice(a * lanes, (a + 1) * lanes)
        source = group_place(far_pairs[1:2, across])
        source_out[where, :] = jnp.where(
            lane % rank < spread(rank_ref[a : a + 1, :]), spread(source), -1
        )
        target_out[where, :] = spread(far_pairs[0:1, across] - recv_index * group_rows).astype(f32)


def far_part(source_ref, target_ref, deficit_ref, v_buf, u_buf, out_ref, before):
    factor_rows = v_buf.shape[0]
    part = factor_rows // chunks
    source_count = deficit_ref.shape[0]
    target_count = out_ref.shape[0]
    deficit = deficit_ref[...]
    source_ids = lax.broadcasted_iota(jnp.int32, (source_count, lanes), 0)
    target_ids = [
        (lax.broadcasted_iota(jnp.int32, (16, lanes), 0) + 16 * k).astype(f32).astype(bf16)
        for k in range(target_count // 16)
    ]
    out_ref[...] = jnp.zeros_like(out_ref)

    step = 0
    for body in bodies:
        for i in range(step, step + body):
            before(i)
        base, count = step * part, body * part
        products = lax.dot_general(
            deficit, v_buf[base : base + count, :], by_row, preferred_element_type=f32
        )
        spread = []
        for k in range(count // lanes):
            row = base // lanes + k
            source = source_ref[row : row + 1, :]
            target = jnp.broadcast_to(target_ref[row : row + 1, :], (16, lanes)).astype(bf16)
            coef = jnp.sum(
                jnp.where(source_ids == source, products[:, k * lanes : (k + 1) * lanes], 0.0),
                axis=0,
                keepdims=True,
            )
            coef = jnp.broadcast_to(coef, (16, lanes)).astype(bf16)
            spread.append(
                jnp.concatenate(
                    [jnp.where(ids == target, coef, jnp.zeros_like(coef)) for ids in target_ids], 0
                )
            )
        out_ref[...] += jnp.dot(
            jnp.concatenate(spread, 1), u_buf[base : base + count, :], preferred_element_type=f32
        )
        step += body


def near_part(hot_ref, target_ref, columns_ref, tiles_hbm, tile_buf, sems, count):
    tile_count = tile_buf.shape[0]
    part = tile_count // near_chunks
    copies = [
        pltpu.make_async_copy(
            tiles_hbm.at[i * part : (i + 1) * part], tile_buf.at[i * part : (i + 1) * part], sems.at[i]
        )
        for i in range(near_chunks)
    ]
    for copy in copies:
        copy.start()
    deficits = jnp.dot(hot_ref[...], columns_ref[...], preferred_element_type=f32)
    ids = lax.broadcasted_iota(jnp.int32, (count, lanes), 0)
    total = jnp.zeros((count, lanes), f32)
    for i, copy in enumerate(copies):
        copy.wait()
        for t in range(i * part, (i + 1) * part):
            placed = jnp.where(ids == target_ref[t : t + 1, :], deficits[t : t + 1, :], 0.0).astype(bf16)
            total += lax.dot_general(placed, tile_buf[t], by_row, preferred_element_type=f32)
    return total


def far_stream(source_ref, target_ref, deficit_ref, v_hbm, u_hbm, out_ref, v_buf, u_buf, sems):
    part = v_hbm.shape[0] // chunks

    def copies(i):
        where = pl.ds(pl.multiple_of(i * part, part), part)
        return (
            pltpu.make_async_copy(v_hbm.at[where], v_buf.at[where], sems.at[0, i]),
            pltpu.make_async_copy(u_hbm.at[where], u_buf.at[where], sems.at[1, i]),
        )

    for i in range(chunks):
        for copy in copies(i):
            copy.start()

    def before(i):
        for copy in copies(i):
            copy.wait()

    far_part(source_ref, target_ref, deficit_ref, v_buf, u_buf, out_ref, before)


def far_kernel(source_ref, target_ref, deficit_ref, v_hbm, u_hbm, out_ref, v_buf, u_buf, sems):
    far_stream(source_ref, target_ref, deficit_ref, v_hbm, u_hbm, out_ref, v_buf, u_buf, sems)


def far_send_kernel(
    source_ref, target_ref, deficit_ref, v_hbm, u_hbm, out_ref, v_buf, u_buf, sems, total_ref
):
    far_stream(source_ref, target_ref, deficit_ref, v_hbm, u_hbm, total_ref, v_buf, u_buf, sems)
    out_ref[...] = total_ref[...].astype(bf16)


def near_kernel(hot_ref, target_ref, columns_ref, tiles_hbm, out_ref, tile_buf, sems):
    count = out_ref.shape[0]
    out_ref[...] = near_part(hot_ref, target_ref, columns_ref, tiles_hbm, tile_buf, sems, count)


def near_send_kernel(
    hot_ref, target_ref, columns_ref, tiles_hbm, far_ref, out_ref, tile_buf, sems, total_ref
):
    count = out_ref.shape[1]
    near = near_part(hot_ref, target_ref, columns_ref, tiles_hbm, tile_buf, sems, count)
    total_ref[...] = far_ref[...]
    own = pl.ds(pl.multiple_of(lax.axis_index("src") * count, count), count)
    total_ref[own, :] += near
    total = total_ref[...].astype(bf16).reshape(-1, count, lanes)
    groups = total.shape[0]
    for k in range(out_ref.shape[0] // groups):
        out_ref[k * groups : (k + 1) * groups] = total


def join_kernel(*refs):
    parts, (columns_ref, send_ref) = refs[:-2], refs[-2:]
    columns = jnp.concatenate([part[3] for part in parts], 0).astype(bf16)
    columns_ref[...] = columns
    for k in range(send_ref.shape[0]):
        send_ref[k] = columns


def update_kernel(stress_ref, *refs):
    parts, (columns_ref, send_ref, own_ref) = refs[:-3], refs[-3:]
    group = stress_ref.shape[0] // len(parts)
    columns = []
    for k, part in enumerate(parts):
        first = (lax.axis_index("recv") ^ k) * group
        stress = stress_ref[first].astype(f32)
        for b in range(1, group):
            stress += stress_ref[first + b].astype(f32)
        if k == 0:
            own_ref[...] = stress
        columns.append(part[2] - jnp.exp(part[0] + part[1] * stress))
    columns = jnp.concatenate(columns, 0).astype(bf16)
    columns_ref[...] = columns
    for k in range(send_ref.shape[0]):
        send_ref[k] = columns


def final_kernel(own_ref, first_ref, second_ref, near_ref, order_ref, p_out, q_out):
    p, q, a, b, slip, plate, theta_rate, gain = [own_ref[k] for k in range(8)]
    first_p = (first_ref[...] - b * theta_rate) * gain
    speed = jnp.exp(p + time_step * first_p)
    second_q = jnp.exp(-(q + time_step * theta_rate)) - speed / slip
    stress = jnp.sum(second_ref[...].astype(f32), axis=0) + near_ref[...]
    second_p = (stress - b * second_q) / (a + damping * speed)
    new_p = p + 0.5 * time_step * (first_p + second_p)
    new_q = q + 0.5 * time_step * (theta_rate + second_q)
    pieces = []
    for value in (new_p, new_q):
        for _ in range(3):
            piece = value.astype(bf16).astype(f32)
            value = value - piece
            pieces.append(piece)
    rows = p.shape[0]
    order = order_ref[...]
    row, lane = order // lanes, order % lanes
    row_ids = lax.broadcasted_iota(jnp.int32, (rows, lanes), 0)
    lane_ids = lax.broadcasted_iota(jnp.int32, (lanes, lanes), 0)
    total = jnp.zeros((len(pieces) * rows, lanes), f32)
    for r in range(rows):
        here = row_ids == row[r : r + 1, :]
        placed = jnp.concatenate(
            [jnp.where(here, piece[r : r + 1, :], 0.0) for piece in pieces], 0
        ).astype(bf16)
        spread = jnp.where(lane_ids == lane[r : r + 1, :], 1.0, 0.0).astype(bf16)
        total += lax.dot_general(placed, spread, by_row, preferred_element_type=f32)
    for k, out in enumerate((p_out, q_out)):
        high, mid, low = [total[(3 * k + j) * rows : (3 * k + j + 1) * rows, :] for j in range(3)]
        out[...] = (low + mid) + high


def on_device(
    log_rate,
    log_state,
    a_sigma,
    b_sigma,
    crit_slip,
    plate_rate,
    cluster_order,
    near_tiles,
    near_pairs,
    far_u,
    far_v,
    far_pairs,
    far_ranks,
):
    src_count = lax.axis_size("src")
    recv_count = lax.axis_size("recv")
    device_count = src_count * recv_count
    tile_count = near_tiles.shape[0]
    own_clusters = log_rate.shape[0] // lanes
    group_rows = own_clusters * src_count
    source_rows = own_clusters * recv_count
    far_count, rank = far_u.shape[:2]
    factor_rows = far_count * rank
    params = pltpu.CompilerParams(vmem_limit_bytes=vmem_bytes)
    whole = (own_clusters, lanes)

    arguments = [x.reshape(whole) for x in (log_rate, log_state, a_sigma, b_sigma, crit_slip, plate_rate)]
    own, shared, order = pl.pallas_call(
        order_kernel,
        in_specs=[anywhere] * 7,
        out_specs=(in_vmem,) * 3,
        out_shape=(
            jax.ShapeDtypeStruct((8,) + whole, f32),
            jax.ShapeDtypeStruct((4,) + whole, f32),
            jax.ShapeDtypeStruct(whole, jnp.int32),
        ),
        scratch_shapes=[
            pltpu.VMEM((6,) + whole, f32),
            pltpu.VMEM(whole, jnp.int32),
            pltpu.SemaphoreType.DMA((7,)),
        ],
        compiler_params=params,
    )(*[in_hbm(x) for x in arguments + [cluster_order.reshape(whole)]])

    parts = [shared] + [
        lax.ppermute(shared, "recv", [(i, i ^ k) for i in range(recv_count)])
        for k in range(1, recv_count)
    ]
    columns_shape = jax.ShapeDtypeStruct((source_rows, lanes), bf16)
    send_shape = jax.ShapeDtypeStruct((src_count, source_rows, lanes), bf16)
    first_columns, first_send = pl.pallas_call(
        join_kernel, out_shape=(columns_shape, send_shape), compiler_params=params
    )(*parts)
    all_first = lax.all_to_all(first_send, "src", split_axis=0, concat_axis=0, tiled=True)

    table = (factor_rows // lanes, lanes)
    hot = (tile_count, own_clusters * device_count)
    source_table, target_table, near_hot, near_target = pl.pallas_call(
        functools.partial(table_kernel, rank=rank, own_clusters=own_clusters, src_count=src_count),
        in_specs=[in_smem, anywhere, anywhere],
        out_specs=(in_vmem,) * 4,
        out_shape=(
            jax.ShapeDtypeStruct(table, jnp.int32),
            jax.ShapeDtypeStruct(table, f32),
            jax.ShapeDtypeStruct(hot, bf16),
            jax.ShapeDtypeStruct((tile_count, lanes), jnp.int32),
        ),
        scratch_shapes=[
            pltpu.VMEM(far_pairs.shape, jnp.int32),
            pltpu.VMEM((far_count // lanes, lanes), jnp.int32),
            pltpu.VMEM(hot, f32),
            pltpu.SemaphoreType.DMA((2,)),
        ],
        compiler_params=params,
    )(near_pairs, in_hbm(far_pairs), in_hbm(far_ranks.reshape(far_count // lanes, lanes)))

    v_rows = in_hbm(far_v.reshape(factor_rows, lanes))
    u_rows = in_hbm(far_u.reshape(factor_rows, lanes))
    far_specs = dict(
        in_specs=[in_vmem] * 3 + [anywhere] * 2,
        out_specs=in_vmem,
        compiler_params=pltpu.CompilerParams(vmem_limit_bytes=far_vmem_bytes),
        cost_estimate=pl.CostEstimate(
            flops=2 * factor_rows * lanes * (source_rows + group_rows), bytes_accessed=2**24, transcendentals=0
        ),
    )
    far_scratch = [
        pltpu.VMEM(v_rows.shape, bf16),
        pltpu.VMEM(u_rows.shape, bf16),
        pltpu.SemaphoreType.DMA((2, chunks)),
    ]
    tiles = in_hbm(near_tiles)
    near_scratch = [pltpu.VMEM(near_tiles.shape, bf16), pltpu.SemaphoreType.DMA((near_chunks,))]
    total_scratch = pltpu.VMEM((group_rows, lanes), f32)

    first_far = pl.pallas_call(
        far_kernel,
        out_shape=jax.ShapeDtypeStruct((group_rows, lanes), f32),
        scratch_shapes=far_scratch,
        **far_specs,
    )(source_table, target_table, first_columns, v_rows, u_rows)
    partial = pl.pallas_call(
        near_send_kernel,
        in_specs=[in_vmem] * 3 + [anywhere, in_vmem],
        out_specs=in_vmem,
        out_shape=jax.ShapeDtypeStruct((device_count,) + whole, bf16),
        scratch_shapes=near_scratch + [total_scratch],
        compiler_params=params,
    )(near_hot, near_target, all_first.reshape(-1, lanes), tiles, first_far)
    stress_parts = lax.all_to_all(partial, ("recv", "src"), split_axis=0, concat_axis=0, tiled=True)

    second_columns, second_send, first_stress = pl.pallas_call(
        update_kernel,
        in_specs=[in_vmem] * (1 + recv_count),
        out_specs=(in_vmem, in_vmem, in_vmem),
        out_shape=(columns_shape, send_shape, jax.ShapeDtypeStruct(whole, f32)),
        compiler_params=params,
    )(stress_parts, *parts)
    all_second = lax.all_to_all(second_send, "src", split_axis=0, concat_axis=0, tiled=True)
    second_far = pl.pallas_call(
        far_send_kernel,
        out_shape=jax.ShapeDtypeStruct((group_rows, lanes), bf16),
        scratch_shapes=far_scratch + [total_scratch],
        **far_specs,
    )(source_table, target_table, second_columns, v_rows, u_rows)
    second_parts = lax.all_to_all(
        second_far.reshape((src_count,) + whole), "src", split_axis=0, concat_axis=0, tiled=True
    )
    second_near = pl.pallas_call(
        near_kernel,
        in_specs=[in_vmem] * 3 + [anywhere],
        out_specs=in_vmem,
        out_shape=jax.ShapeDtypeStruct(whole, f32),
        scratch_shapes=near_scratch,
        compiler_params=params,
    )(near_hot, near_target, all_second.reshape(-1, lanes), tiles)
    new_p, new_q = pl.pallas_call(
        final_kernel,
        out_shape=(jax.ShapeDtypeStruct(whole, f32), jax.ShapeDtypeStruct(whole, f32)),
        compiler_params=params,
    )(own, first_stress, second_parts, second_near, order)
    return new_p.reshape(-1), new_q.reshape(-1)


def solution(mesh):
    return jax.shard_map(
        on_device,
        mesh=mesh,
        in_specs=(
            P(("recv", "src")),
            P(("recv", "src")),
            P(("recv", "src")),
            P(("recv", "src")),
            P(("recv", "src")),
            P(("recv", "src")),
            P(("recv", "src"), None),
            P(("recv", "src"), None, None),
            P(None, "recv"),
            P(("recv", "src"), None, None),
            P(("recv", "src"), None, None),
            P(None, ("recv", "src")),
            P(("recv", "src")),
        ),
        out_specs=(P(("recv", "src")), P(("recv", "src"))),
        check_vma=False,
    )
```

```python
import functools

import jax
import jax.numpy as jnp
from jax import lax
from jax.experimental import pallas as pl
from jax.experimental.pallas import tpu as pltpu
from jax.sharding import PartitionSpec as P

time_step = 0.1
damping = 0.5
f32 = jnp.float32
bf16 = jnp.bfloat16
lanes = 128
chunks = 8
code_base = 4096
vmem_bytes = 8 * 2**20
far_vmem_bytes = 28 * 2**20
bodies = (1, 2, 2, 2, 1)
by_row = (((1,), (1,)), ((), ()))
in_vmem = pl.BlockSpec(memory_space=pltpu.VMEM)
anywhere = pl.BlockSpec(memory_space=pl.ANY)
in_smem = pl.BlockSpec(memory_space=pltpu.SMEM)


def in_hbm(x):
    return pltpu.with_memory_space_constraint(x, pltpu.HBM)


def order_kernel(*refs):
    arguments, (own_ref, deficit_ref, order_out, buf, order_buf, sems) = refs[:7], refs[7:]
    count = len(arguments) - 1
    copies = [
        pltpu.make_async_copy(ref, order_buf if k == count else buf.at[k], sems.at[k])
        for k, ref in enumerate(arguments)
    ]
    for copy in copies:
        copy.start()
    for copy in copies:
        copy.wait()
    order = order_buf[...]
    order_out[...] = order
    row, lane = order // lanes, order % lanes
    rows = order.shape[0]
    sorted_values = [jnp.zeros(order.shape, f32)] * count
    for r in range(rows):
        here = row == r
        for k in range(count):
            spread = jnp.broadcast_to(buf[k, r : r + 1, :], order.shape)
            got = jnp.take_along_axis(spread, lane, axis=1)
            sorted_values[k] = jnp.where(here, got, sorted_values[k])
    p, q, a, b, slip, plate = sorted_values
    speed = jnp.exp(p)
    theta_rate = jnp.exp(-q) - speed / slip
    gain = 1.0 / (a + damping * speed)
    for k, value in enumerate((p, q, a, b, slip, plate, theta_rate, gain)):
        own_ref[k] = value
    deficit_ref[...] = (plate - speed).astype(bf16)


def table_kernel(
    near_pairs, far_pairs_hbm, rank_hbm, far_out, near_out, far_pairs, rank_ref, sems, *, rank, own_clusters, src_count
):
    copies = (
        pltpu.make_async_copy(far_pairs_hbm, far_pairs, sems.at[0]),
        pltpu.make_async_copy(rank_hbm, rank_ref, sems.at[1]),
    )
    for copy in copies:
        copy.start()
    recv_index, src_index = lax.axis_index("recv"), lax.axis_index("src")
    group_rows = own_clusters * src_count
    source_rows = own_clusters * lax.axis_size("recv")

    def group_place(cluster):
        return ((cluster // group_rows) ^ recv_index) * own_clusters + cluster % own_clusters

    tile_count = near_out.shape[0]
    first_own = recv_index * group_rows + src_index * own_clusters
    for t in range(tile_count):
        target = near_pairs[0, src_index * tile_count + t] - first_own
        source = near_pairs[1, src_index * tile_count + t]
        place = (source // own_clusters) % src_count * source_rows + group_place(source)
        near_out[t : t + 1, :] = jnp.full((1, lanes), target * code_base + place, jnp.int32)

    for copy in copies:
        copy.wait()
    per_row = lanes // rank
    group = lanes // per_row
    shape = (group, lanes)
    lane = lax.broadcasted_iota(jnp.int32, shape, 1)
    pick = lax.broadcasted_iota(jnp.int32, shape, 0) * per_row + lane // rank

    def spread(row):
        return jnp.take_along_axis(jnp.broadcast_to(row, shape), pick, axis=1)

    for a in range(rank_ref.shape[0]):
        across = slice(a * lanes, (a + 1) * lanes)
        target = (far_pairs[0:1, across] - recv_index * group_rows) * code_base
        source = spread(target + group_place(far_pairs[1:2, across]))
        missing = spread(target + (code_base - 1))
        far_out[a * group : (a + 1) * group, :] = jnp.where(
            lane % rank < spread(rank_ref[a : a + 1, :]), source, missing
        )


def far_part(code_ref, deficit, v_buf, u_buf, out_ref, before):
    factor_rows = v_buf.shape[0]
    part = factor_rows // chunks
    source_count = deficit.shape[0]
    target_count = out_ref.shape[0]
    source_ids = lax.broadcasted_iota(jnp.int32, (source_count, lanes), 0)
    target_ids = [
        (lax.broadcasted_iota(jnp.int32, (16, lanes), 0) + 16 * k).astype(f32).astype(bf16)
        for k in range(target_count // 16)
    ]
    out_ref[...] = jnp.zeros_like(out_ref)

    step = 0
    for body in bodies:
        for i in range(step, step + body):
            before(i)
        base, count = step * part, body * part
        products = lax.dot_general(
            deficit, v_buf[base : base + count, :], by_row, preferred_element_type=f32
        )
        spread = []
        for k in range(count // lanes):
            row = base // lanes + k
            code = code_ref[row : row + 1, :]
            source = code % code_base
            target = jnp.broadcast_to((code // code_base).astype(f32), (16, lanes)).astype(bf16)
            coef = jnp.sum(
                jnp.where(source_ids == source, products[:, k * lanes : (k + 1) * lanes], 0.0),
                axis=0,
                keepdims=True,
            )
            coef = jnp.broadcast_to(coef, (16, lanes)).astype(bf16)
            spread.append(
                jnp.concatenate(
                    [jnp.where(ids == target, coef, jnp.zeros_like(coef)) for ids in target_ids], 0
                )
            )
        out_ref[...] += jnp.dot(
            jnp.concatenate(spread, 1), u_buf[base : base + count, :], preferred_element_type=f32
        )
        step += body


def far_kernel(code_ref, *refs):
    parts, (v_hbm, u_hbm, out_ref, v_buf, u_buf, sems, total_ref) = refs[:-7], refs[-7:]
    part = v_hbm.shape[0] // chunks

    def copies(i):
        where = slice(i * part, (i + 1) * part)
        return (
            pltpu.make_async_copy(v_hbm.at[where], v_buf.at[where], sems.at[0, i]),
            pltpu.make_async_copy(u_hbm.at[where], u_buf.at[where], sems.at[1, i]),
        )

    for i in range(chunks):
        for copy in copies(i):
            copy.start()

    def before(i):
        for copy in copies(i):
            copy.wait()

    deficit = jnp.concatenate([ref[...] for ref in parts], 0)
    count = parts[0].shape[0]
    for k in range(out_ref.shape[0]):
        out_ref[k, count:, :] = deficit
    far_part(code_ref, deficit, v_buf, u_buf, total_ref, before)
    for k in range(out_ref.shape[0]):
        out_ref[k, :count, :] = total_ref[k * count : (k + 1) * count, :].astype(bf16)


def whole_stress(code_ref, came_ref, tile_ref, count):
    senders = came_ref.shape[0]
    columns = jnp.concatenate([came_ref[k, count:, :] for k in range(senders)], 0)
    tile_count = tile_ref.shape[0]
    code = code_ref[...]
    place, target = code % code_base, code // code_base
    place_ids = lax.broadcasted_iota(jnp.int32, (tile_count, lanes), 1)
    deficits = jnp.zeros((tile_count, lanes), f32)
    for k in range(columns.shape[0] // lanes):
        hot = jnp.where(place_ids + k * lanes == place, 1.0, 0.0).astype(bf16)
        deficits += jnp.dot(hot, columns[k * lanes : (k + 1) * lanes, :], preferred_element_type=f32)
    ids = lax.broadcasted_iota(jnp.int32, (count, lanes), 0)
    placed = [
        jnp.where(ids == target[t : t + 1, :], deficits[t : t + 1, :], 0.0).astype(bf16)
        for t in range(tile_count)
    ]
    near = lax.dot_general(
        jnp.concatenate(placed, 1),
        jnp.concatenate([tile_ref[t] for t in range(tile_count)], 1),
        by_row,
        preferred_element_type=f32,
    )
    far = came_ref[0, :count, :].astype(f32)
    for k in range(1, senders):
        far += came_ref[k, :count, :].astype(f32)
    return far + near


def first_kernel(code_ref, came_ref, tile_ref, own_ref, stress_ref, deficit_ref):
    stress = whole_stress(code_ref, came_ref, tile_ref, stress_ref.shape[0])
    stress_ref[...] = stress
    p, b, plate, theta_rate, gain = [own_ref[k] for k in (0, 3, 5, 6, 7)]
    speed = jnp.exp(p + time_step * ((stress - b * theta_rate) * gain))
    deficit_ref[...] = (plate - speed).astype(bf16)


def final_kernel(code_ref, came_ref, tile_ref, own_ref, first_ref, order_ref, p_out, q_out):
    stress = whole_stress(code_ref, came_ref, tile_ref, first_ref.shape[0])
    p, q, a, b, slip, plate, theta_rate, gain = [own_ref[k] for k in range(8)]
    first_p = (first_ref[...] - b * theta_rate) * gain
    speed = jnp.exp(p + time_step * first_p)
    second_q = jnp.exp(-(q + time_step * theta_rate)) - speed / slip
    second_p = (stress - b * second_q) / (a + damping * speed)
    new_p = p + 0.5 * time_step * (first_p + second_p)
    new_q = q + 0.5 * time_step * (theta_rate + second_q)
    pieces = []
    for value in (new_p, new_q):
        for _ in range(3):
            piece = value.astype(bf16).astype(f32)
            value = value - piece
            pieces.append(piece)
    rows = p.shape[0]
    order = order_ref[...]
    row, lane = order // lanes, order % lanes
    row_ids = lax.broadcasted_iota(jnp.int32, (rows, lanes), 0)
    lane_ids = lax.broadcasted_iota(jnp.int32, (lanes, lanes), 0)
    total = jnp.zeros((len(pieces) * rows, lanes), f32)
    for r in range(rows):
        here = row_ids == row[r : r + 1, :]
        placed = jnp.concatenate(
            [jnp.where(here, piece[r : r + 1, :], 0.0) for piece in pieces], 0
        ).astype(bf16)
        spread = jnp.where(lane_ids == lane[r : r + 1, :], 1.0, 0.0).astype(bf16)
        total += lax.dot_general(placed, spread, by_row, preferred_element_type=f32)
    for k, out in enumerate((p_out, q_out)):
        high, mid, low = [total[(3 * k + j) * rows : (3 * k + j + 1) * rows, :] for j in range(3)]
        out[...] = (low + mid) + high


def on_device(
    log_rate,
    log_state,
    a_sigma,
    b_sigma,
    crit_slip,
    plate_rate,
    cluster_order,
    near_tiles,
    near_pairs,
    far_u,
    far_v,
    far_pairs,
    far_ranks,
):
    src_count = lax.axis_size("src")
    recv_count = lax.axis_size("recv")
    device_count = src_count * recv_count
    tile_count = near_tiles.shape[0]
    own_clusters = log_rate.shape[0] // lanes
    group_rows = own_clusters * src_count
    source_rows = own_clusters * recv_count
    far_count, rank = far_u.shape[:2]
    factor_rows = far_count * rank
    params = pltpu.CompilerParams(vmem_limit_bytes=vmem_bytes)
    whole = (own_clusters, lanes)

    arguments = [x.reshape(whole) for x in (log_rate, log_state, a_sigma, b_sigma, crit_slip, plate_rate)]
    own, first_deficit, order = pl.pallas_call(
        order_kernel,
        in_specs=[anywhere] * 7,
        out_specs=(in_vmem,) * 3,
        out_shape=(
            jax.ShapeDtypeStruct((8,) + whole, f32),
            jax.ShapeDtypeStruct(whole, bf16),
            jax.ShapeDtypeStruct(whole, jnp.int32),
        ),
        scratch_shapes=[
            pltpu.VMEM((6,) + whole, f32),
            pltpu.VMEM(whole, jnp.int32),
            pltpu.SemaphoreType.DMA((7,)),
        ],
        compiler_params=params,
    )(*[in_hbm(x) for x in arguments + [cluster_order.reshape(whole)]])

    far_codes, near_codes = pl.pallas_call(
        functools.partial(table_kernel, rank=rank, own_clusters=own_clusters, src_count=src_count),
        in_specs=[in_smem, anywhere, anywhere],
        out_specs=(in_vmem,) * 2,
        out_shape=(
            jax.ShapeDtypeStruct((factor_rows // lanes, lanes), jnp.int32),
            jax.ShapeDtypeStruct((tile_count, lanes), jnp.int32),
        ),
        scratch_shapes=[
            pltpu.VMEM(far_pairs.shape, jnp.int32),
            pltpu.VMEM((far_count // lanes, lanes), jnp.int32),
            pltpu.SemaphoreType.DMA((2,)),
        ],
        compiler_params=params,
    )(near_pairs, in_hbm(far_pairs), in_hbm(far_ranks.reshape(far_count // lanes, lanes)))

    v_rows = in_hbm(far_v.reshape(factor_rows, lanes))
    u_rows = in_hbm(far_u.reshape(factor_rows, lanes))

    def exchange(deficit):
        parts = [deficit] + [
            lax.ppermute(deficit, "recv", [(i, i ^ k) for i in range(recv_count)])
            for k in range(1, recv_count)
        ]
        send = pl.pallas_call(
            far_kernel,
            in_specs=[in_vmem] * (1 + recv_count) + [anywhere] * 2,
            out_specs=in_vmem,
            out_shape=jax.ShapeDtypeStruct((src_count, own_clusters + source_rows, lanes), bf16),
            scratch_shapes=[
                pltpu.VMEM(v_rows.shape, bf16),
                pltpu.VMEM(u_rows.shape, bf16),
                pltpu.SemaphoreType.DMA((2, chunks)),
                pltpu.VMEM((group_rows, lanes), f32),
            ],
            compiler_params=pltpu.CompilerParams(vmem_limit_bytes=far_vmem_bytes),
            cost_estimate=pl.CostEstimate(
                flops=2 * factor_rows * lanes * (source_rows + group_rows), bytes_accessed=2**24, transcendentals=0
            ),
        )(far_codes, *parts, v_rows, u_rows)
        return lax.all_to_all(send, "src", split_axis=0, concat_axis=0, tiled=True)

    first_stress, second_deficit = pl.pallas_call(
        first_kernel,
        in_specs=[in_vmem] * 4,
        out_specs=(in_vmem,) * 2,
        out_shape=(jax.ShapeDtypeStruct(whole, f32), jax.ShapeDtypeStruct(whole, bf16)),
        compiler_params=params,
    )(near_codes, exchange(first_deficit), near_tiles, own)
    new_p, new_q = pl.pallas_call(
        final_kernel,
        out_shape=(jax.ShapeDtypeStruct(whole, f32), jax.ShapeDtypeStruct(whole, f32)),
        compiler_params=params,
    )(near_codes, exchange(second_deficit), near_tiles, own, first_stress, order)
    return new_p.reshape(-1), new_q.reshape(-1)


def solution(mesh):
    return jax.shard_map(
        on_device,
        mesh=mesh,
        in_specs=(
            P(("recv", "src")),
            P(("recv", "src")),
            P(("recv", "src")),
            P(("recv", "src")),
            P(("recv", "src")),
            P(("recv", "src")),
            P(("recv", "src"), None),
            P(("recv", "src"), None, None),
            P(None, "recv"),
            P(("recv", "src"), None, None),
            P(("recv", "src"), None, None),
            P(None, ("recv", "src")),
            P(("recv", "src")),
        ),
        out_specs=(P(("recv", "src")), P(("recv", "src"))),
        check_vma=False,
    )
```

```python
import functools

import jax
import jax.numpy as jnp
from jax import lax
from jax.experimental import pallas as pl
from jax.experimental.pallas import tpu as pltpu
from jax.sharding import PartitionSpec as P

time_step = 0.1
damping = 0.5
f32 = jnp.float32
bf16 = jnp.bfloat16
lanes = 128
chunks = 8
code_base = 4096
vmem_bytes = 8 * 2**20
far_vmem_bytes = 28 * 2**20
bodies = (1, 2, 2, 2, 1)
by_row = (((1,), (1,)), ((), ()))
in_vmem = pl.BlockSpec(memory_space=pltpu.VMEM)
anywhere = pl.BlockSpec(memory_space=pl.ANY)


def in_hbm(x):
    return pltpu.with_memory_space_constraint(x, pltpu.HBM)


def order_kernel(*refs):
    arguments, (own_ref, deficit_ref, order_out, buf, order_buf, sems) = refs[:7], refs[7:]
    count = len(arguments) - 1
    copies = [
        pltpu.make_async_copy(ref, order_buf if k == count else buf.at[k], sems.at[k])
        for k, ref in enumerate(arguments)
    ]
    for copy in copies:
        copy.start()
    for copy in copies:
        copy.wait()
    order = order_buf[...]
    order_out[...] = order
    row, lane = order // lanes, order % lanes
    rows = order.shape[0]
    sorted_values = [jnp.zeros(order.shape, f32)] * count
    for r in range(rows):
        here = row == r
        for k in range(count):
            spread = jnp.broadcast_to(buf[k, r : r + 1, :], order.shape)
            got = jnp.take_along_axis(spread, lane, axis=1)
            sorted_values[k] = jnp.where(here, got, sorted_values[k])
    p, q, a, b, slip, plate = sorted_values
    speed = jnp.exp(p)
    theta_rate = jnp.exp(-q) - speed / slip
    gain = 1.0 / (a + damping * speed)
    for k, value in enumerate((p, q, a, b, slip, plate, theta_rate, gain)):
        own_ref[k] = value
    deficit_ref[...] = (plate - speed).astype(bf16)


def table_kernel(
    near_hbm, far_hbm, rank_hbm, far_out, near_out, pick_out, near_pairs, far_pairs, rank_ref, sems, *,
    rank, own_clusters, src_count, capacity,
):
    copies = [
        pltpu.make_async_copy(there, here, sems.at[k])
        for k, (there, here) in enumerate(((near_hbm, near_pairs), (far_hbm, far_pairs), (rank_hbm, rank_ref)))
    ]
    for copy in copies:
        copy.start()
    recv_index, src_index = lax.axis_index("recv"), lax.axis_index("src")
    group_rows = own_clusters * src_count
    source_rows = own_clusters * lax.axis_size("recv")

    def group_place(cluster):
        return ((cluster // group_rows) ^ recv_index) * own_clusters + cluster % own_clusters

    for copy in copies:
        copy.wait()
    tile_count = near_out.shape[0]
    padding = jnp.full((1, lanes - tile_count), -1, jnp.int32)

    def by_device(row):
        return jnp.concatenate(
            [
                jnp.concatenate([near_pairs[row : row + 1, k * tile_count : (k + 1) * tile_count], padding], 1)
                for k in range(src_count)
            ],
            0,
        )

    target, source = by_device(0), by_device(1)
    group = jnp.where(source < 0, -1, (source // own_clusters) % src_count)
    place = jnp.where(source < 0, -1, group_place(source))
    same = [group == g for g in range(src_count)]
    before = lax.broadcasted_iota(jnp.int32, (lanes, lanes), 0) < lax.broadcasted_iota(jnp.int32, (lanes, lanes), 1)
    counts = jnp.dot(
        jnp.concatenate([jnp.where(here, 1.0, 0.0) for here in same], 0).astype(bf16),
        jnp.where(before, 1.0, 0.0).astype(bf16),
        preferred_element_type=f32,
    )
    slot = jnp.zeros(source.shape, f32)
    for g, here in enumerate(same):
        slot += jnp.where(here, counts[g * src_count : (g + 1) * src_count, :], 0.0)
    slot = slot.astype(jnp.int32)
    sent = jnp.where(group == src_index, slot, -1)
    slot_ids = lax.broadcasted_iota(jnp.int32, (capacity, lanes), 0)
    place_ids = lax.broadcasted_iota(jnp.int32, (source_rows, lanes), 0)
    for k in range(src_count):
        from_slot = jnp.where(slot_ids == sent[k : k + 1, :], 1.0, 0.0).astype(bf16)
        from_place = jnp.where(place_ids == place[k : k + 1, :], 1.0, 0.0).astype(bf16)
        pick_out[k * capacity : (k + 1) * capacity, :] = lax.dot_general(
            from_slot, from_place, by_row, preferred_element_type=f32
        ).astype(bf16)
    first_own = recv_index * group_rows + src_index * own_clusters
    code = (target - first_own) * code_base + group * capacity + slot
    own = lax.broadcasted_iota(jnp.int32, code.shape, 0) == src_index
    code = jnp.sum(jnp.where(own, code.astype(f32), 0.0), axis=0, keepdims=True)
    near_out[...] = jnp.transpose(jnp.broadcast_to(code, (lanes, lanes))).astype(jnp.int32)[:tile_count, :]

    per_row = lanes // rank
    group = lanes // per_row
    shape = (group, lanes)
    lane = lax.broadcasted_iota(jnp.int32, shape, 1)
    pick = lax.broadcasted_iota(jnp.int32, shape, 0) * per_row + lane // rank

    def spread(row):
        return jnp.take_along_axis(jnp.broadcast_to(row, shape), pick, axis=1)

    for a in range(rank_ref.shape[0]):
        across = slice(a * lanes, (a + 1) * lanes)
        target = (far_pairs[0:1, across] - recv_index * group_rows) * code_base
        source = spread(target + group_place(far_pairs[1:2, across]))
        missing = spread(target + (code_base - 1))
        far_out[a * group : (a + 1) * group, :] = jnp.where(
            lane % rank < spread(rank_ref[a : a + 1, :]), source, missing
        )


def far_part(code_ref, deficit, v_buf, u_buf, out_ref, before):
    factor_rows = v_buf.shape[0]
    part = factor_rows // chunks
    source_count = deficit.shape[0]
    target_count = out_ref.shape[0]
    source_ids = lax.broadcasted_iota(jnp.int32, (source_count, lanes), 0)
    target_ids = [
        (lax.broadcasted_iota(jnp.int32, (16, lanes), 0) + 16 * k).astype(f32).astype(bf16)
        for k in range(target_count // 16)
    ]
    out_ref[...] = jnp.zeros_like(out_ref)

    step = 0
    for body in bodies:
        for i in range(step, step + body):
            before(i)
        base, count = step * part, body * part
        products = lax.dot_general(
            deficit, v_buf[base : base + count, :], by_row, preferred_element_type=f32
        )
        spread = []
        for k in range(count // lanes):
            row = base // lanes + k
            code = code_ref[row : row + 1, :]
            source = code % code_base
            target = jnp.broadcast_to((code // code_base).astype(f32), (16, lanes)).astype(bf16)
            coef = jnp.sum(
                jnp.where(source_ids == source, products[:, k * lanes : (k + 1) * lanes], 0.0),
                axis=0,
                keepdims=True,
            )
            coef = jnp.broadcast_to(coef, (16, lanes)).astype(bf16)
            spread.append(
                jnp.concatenate(
                    [jnp.where(ids == target, coef, jnp.zeros_like(coef)) for ids in target_ids], 0
                )
            )
        out_ref[...] += jnp.dot(
            jnp.concatenate(spread, 1), u_buf[base : base + count, :], preferred_element_type=f32
        )
        step += body


def far_kernel(code_ref, pick_ref, *refs):
    parts, (v_hbm, u_hbm, out_ref, v_buf, u_buf, sems, total_ref) = refs[:-7], refs[-7:]
    part = v_hbm.shape[0] // chunks

    def copies(i):
        where = slice(i * part, (i + 1) * part)
        return (
            pltpu.make_async_copy(v_hbm.at[where], v_buf.at[where], sems.at[0, i]),
            pltpu.make_async_copy(u_hbm.at[where], u_buf.at[where], sems.at[1, i]),
        )

    for i in range(chunks):
        for copy in copies(i):
            copy.start()

    def before(i):
        for copy in copies(i):
            copy.wait()

    deficit = jnp.concatenate([ref[...] for ref in parts], 0)
    count = parts[0].shape[0]
    picked = jnp.dot(pick_ref[...], deficit, preferred_element_type=f32).astype(bf16)
    capacity = out_ref.shape[1] - count
    for k in range(out_ref.shape[0]):
        out_ref[k, count:, :] = picked[k * capacity : (k + 1) * capacity, :]
    far_part(code_ref, deficit, v_buf, u_buf, total_ref, before)
    for k in range(out_ref.shape[0]):
        out_ref[k, :count, :] = total_ref[k * count : (k + 1) * count, :].astype(bf16)


def whole_stress(code_ref, came_ref, tile_ref, count):
    senders = came_ref.shape[0]
    columns = jnp.concatenate([came_ref[k, count:, :] for k in range(senders)], 0)
    tile_count = tile_ref.shape[0]
    code = code_ref[...]
    place, target = code % code_base, code // code_base
    place_ids = lax.broadcasted_iota(jnp.int32, (tile_count, lanes), 1)
    deficits = jnp.zeros((tile_count, lanes), f32)
    for k in range(columns.shape[0] // lanes):
        hot = jnp.where(place_ids + k * lanes == place, 1.0, 0.0).astype(bf16)
        deficits += jnp.dot(hot, columns[k * lanes : (k + 1) * lanes, :], preferred_element_type=f32)
    ids = lax.broadcasted_iota(jnp.int32, (count, lanes), 0)
    placed = [
        jnp.where(ids == target[t : t + 1, :], deficits[t : t + 1, :], 0.0).astype(bf16)
        for t in range(tile_count)
    ]
    near = lax.dot_general(
        jnp.concatenate(placed, 1),
        jnp.concatenate([tile_ref[t] for t in range(tile_count)], 1),
        by_row,
        preferred_element_type=f32,
    )
    far = came_ref[0, :count, :].astype(f32)
    for k in range(1, senders):
        far += came_ref[k, :count, :].astype(f32)
    return far + near


def first_kernel(code_ref, came_ref, tile_ref, own_ref, stress_ref, deficit_ref):
    stress = whole_stress(code_ref, came_ref, tile_ref, stress_ref.shape[0])
    stress_ref[...] = stress
    p, b, plate, theta_rate, gain = [own_ref[k] for k in (0, 3, 5, 6, 7)]
    speed = jnp.exp(p + time_step * ((stress - b * theta_rate) * gain))
    deficit_ref[...] = (plate - speed).astype(bf16)


def final_kernel(code_ref, came_ref, tile_ref, own_ref, first_ref, order_ref, p_out, q_out):
    stress = whole_stress(code_ref, came_ref, tile_ref, first_ref.shape[0])
    p, q, a, b, slip, plate, theta_rate, gain = [own_ref[k] for k in range(8)]
    first_p = (first_ref[...] - b * theta_rate) * gain
    speed = jnp.exp(p + time_step * first_p)
    second_q = jnp.exp(-(q + time_step * theta_rate)) - speed / slip
    second_p = (stress - b * second_q) / (a + damping * speed)
    new_p = p + 0.5 * time_step * (first_p + second_p)
    new_q = q + 0.5 * time_step * (theta_rate + second_q)
    pieces = []
    for value in (new_p, new_q):
        for _ in range(3):
            piece = value.astype(bf16).astype(f32)
            value = value - piece
            pieces.append(piece)
    rows = p.shape[0]
    order = order_ref[...]
    row, lane = order // lanes, order % lanes
    row_ids = lax.broadcasted_iota(jnp.int32, (rows, lanes), 0)
    lane_ids = lax.broadcasted_iota(jnp.int32, (lanes, lanes), 0)
    total = jnp.zeros((len(pieces) * rows, lanes), f32)
    for r in range(rows):
        here = row_ids == row[r : r + 1, :]
        placed = jnp.concatenate(
            [jnp.where(here, piece[r : r + 1, :], 0.0) for piece in pieces], 0
        ).astype(bf16)
        spread = jnp.where(lane_ids == lane[r : r + 1, :], 1.0, 0.0).astype(bf16)
        total += lax.dot_general(placed, spread, by_row, preferred_element_type=f32)
    for k, out in enumerate((p_out, q_out)):
        high, mid, low = [total[(3 * k + j) * rows : (3 * k + j + 1) * rows, :] for j in range(3)]
        out[...] = (low + mid) + high


def on_device(
    log_rate,
    log_state,
    a_sigma,
    b_sigma,
    crit_slip,
    plate_rate,
    cluster_order,
    near_tiles,
    near_pairs,
    far_u,
    far_v,
    far_pairs,
    far_ranks,
):
    src_count = lax.axis_size("src")
    recv_count = lax.axis_size("recv")
    device_count = src_count * recv_count
    tile_count = near_tiles.shape[0]
    own_clusters = log_rate.shape[0] // lanes
    group_rows = own_clusters * src_count
    source_rows = own_clusters * recv_count
    far_count, rank = far_u.shape[:2]
    factor_rows = far_count * rank
    params = pltpu.CompilerParams(vmem_limit_bytes=vmem_bytes)
    whole = (own_clusters, lanes)

    arguments = [x.reshape(whole) for x in (log_rate, log_state, a_sigma, b_sigma, crit_slip, plate_rate)]
    own, first_deficit, order = pl.pallas_call(
        order_kernel,
        in_specs=[anywhere] * 7,
        out_specs=(in_vmem,) * 3,
        out_shape=(
            jax.ShapeDtypeStruct((8,) + whole, f32),
            jax.ShapeDtypeStruct(whole, bf16),
            jax.ShapeDtypeStruct(whole, jnp.int32),
        ),
        scratch_shapes=[
            pltpu.VMEM((6,) + whole, f32),
            pltpu.VMEM(whole, jnp.int32),
            pltpu.SemaphoreType.DMA((7,)),
        ],
        compiler_params=params,
    )(*[in_hbm(x) for x in arguments + [cluster_order.reshape(whole)]])

    capacity = -(-max(2, 2 * tile_count // src_count) // 16) * 16
    far_codes, near_codes, picks = pl.pallas_call(
        functools.partial(
            table_kernel, rank=rank, own_clusters=own_clusters, src_count=src_count, capacity=capacity
        ),
        in_specs=[anywhere] * 3,
        out_specs=(in_vmem,) * 3,
        out_shape=(
            jax.ShapeDtypeStruct((factor_rows // lanes, lanes), jnp.int32),
            jax.ShapeDtypeStruct((tile_count, lanes), jnp.int32),
            jax.ShapeDtypeStruct((src_count * capacity, source_rows), bf16),
        ),
        scratch_shapes=[
            pltpu.VMEM(near_pairs.shape, jnp.int32),
            pltpu.VMEM(far_pairs.shape, jnp.int32),
            pltpu.VMEM((far_count // lanes, lanes), jnp.int32),
            pltpu.SemaphoreType.DMA((3,)),
        ],
        compiler_params=params,
    )(*[in_hbm(x) for x in (near_pairs, far_pairs, far_ranks.reshape(far_count // lanes, lanes))])

    v_rows = in_hbm(far_v.reshape(factor_rows, lanes))
    u_rows = in_hbm(far_u.reshape(factor_rows, lanes))

    def exchange(deficit):
        parts = [deficit] + [
            lax.ppermute(deficit, "recv", [(i, i ^ k) for i in range(recv_count)])
            for k in range(1, recv_count)
        ]
        send = pl.pallas_call(
            far_kernel,
            in_specs=[in_vmem] * (2 + recv_count) + [anywhere] * 2,
            out_specs=in_vmem,
            out_shape=jax.ShapeDtypeStruct((src_count, own_clusters + capacity, lanes), bf16),
            scratch_shapes=[
                pltpu.VMEM(v_rows.shape, bf16),
                pltpu.VMEM(u_rows.shape, bf16),
                pltpu.SemaphoreType.DMA((2, chunks)),
                pltpu.VMEM((group_rows, lanes), f32),
            ],
            compiler_params=pltpu.CompilerParams(vmem_limit_bytes=far_vmem_bytes),
            cost_estimate=pl.CostEstimate(
                flops=2 * factor_rows * lanes * (source_rows + group_rows), bytes_accessed=2**24, transcendentals=0
            ),
        )(far_codes, picks, *parts, v_rows, u_rows)
        return lax.all_to_all(send, "src", split_axis=0, concat_axis=0, tiled=True)

    first_stress, second_deficit = pl.pallas_call(
        first_kernel,
        in_specs=[in_vmem] * 4,
        out_specs=(in_vmem,) * 2,
        out_shape=(jax.ShapeDtypeStruct(whole, f32), jax.ShapeDtypeStruct(whole, bf16)),
        compiler_params=params,
    )(near_codes, exchange(first_deficit), near_tiles, own)
    new_p, new_q = pl.pallas_call(
        final_kernel,
        out_shape=(jax.ShapeDtypeStruct(whole, f32), jax.ShapeDtypeStruct(whole, f32)),
        compiler_params=params,
    )(near_codes, exchange(second_deficit), near_tiles, own, first_stress, order)
    return new_p.reshape(-1), new_q.reshape(-1)


def solution(mesh):
    return jax.shard_map(
        on_device,
        mesh=mesh,
        in_specs=(
            P(("recv", "src")),
            P(("recv", "src")),
            P(("recv", "src")),
            P(("recv", "src")),
            P(("recv", "src")),
            P(("recv", "src")),
            P(("recv", "src"), None),
            P(("recv", "src"), None, None),
            P(None, "recv"),
            P(("recv", "src"), None, None),
            P(("recv", "src"), None, None),
            P(None, ("recv", "src")),
            P(("recv", "src")),
        ),
        out_specs=(P(("recv", "src")), P(("recv", "src"))),
        check_vma=False,
    )
```

```python
import functools

import jax
import jax.numpy as jnp
from jax import lax
from jax.experimental import pallas as pl
from jax.experimental.pallas import tpu as pltpu
from jax.sharding import PartitionSpec as P

time_step = 0.1
damping = 0.5
f32 = jnp.float32
bf16 = jnp.bfloat16
lanes = 128
chunks = 8
code_base = 4096
vmem_bytes = 8 * 2**20
far_vmem_bytes = 28 * 2**20
bodies = (1, 2, 2, 2, 1)
by_row = (((1,), (1,)), ((), ()))
in_vmem = pl.BlockSpec(memory_space=pltpu.VMEM)
anywhere = pl.BlockSpec(memory_space=pl.ANY)


def in_hbm(x):
    return pltpu.with_memory_space_constraint(x, pltpu.HBM)


def order_kernel(*refs):
    arguments, (own_ref, deficit_ref, order_out, buf, order_buf, sems) = refs[:7], refs[7:]
    count = len(arguments) - 1
    copies = [
        pltpu.make_async_copy(ref, order_buf if k == count else buf.at[k], sems.at[k])
        for k, ref in enumerate(arguments)
    ]
    for copy in copies:
        copy.start()
    for copy in copies:
        copy.wait()
    order = order_buf[...]
    order_out[...] = order
    row, lane = order // lanes, order % lanes
    rows = order.shape[0]
    sorted_values = [jnp.zeros(order.shape, f32)] * count
    for r in range(rows):
        here = row == r
        for k in range(count):
            spread = jnp.broadcast_to(buf[k, r : r + 1, :], order.shape)
            got = jnp.take_along_axis(spread, lane, axis=1)
            sorted_values[k] = jnp.where(here, got, sorted_values[k])
    p, q, a, b, slip, plate = sorted_values
    speed = jnp.exp(p)
    theta_rate = jnp.exp(-q) - speed / slip
    gain = 1.0 / (a + damping * speed)
    for k, value in enumerate((p, q, a, b, slip, plate, theta_rate, gain)):
        own_ref[k] = value
    deficit_ref[...] = (plate - speed).astype(bf16)


def head_copies(v_hbm, u_hbm, v_out, u_out, sems):
    copies = [
        pltpu.make_async_copy(there.at[: here.shape[0]], here, sems.at[k])
        for k, (there, here) in enumerate(((v_hbm, v_out), (u_hbm, u_out)))
    ]
    for copy in copies:
        copy.start()
    return copies


def table_kernel(
    near_hbm, far_hbm, rank_hbm, v_hbm, u_hbm, far_out, near_out, pick_out, v_out, u_out,
    near_pairs, far_pairs, rank_ref, sems, head_sems, *,
    rank, own_clusters, src_count, capacity,
):
    copies = [
        pltpu.make_async_copy(there, here, sems.at[k])
        for k, (there, here) in enumerate(((near_hbm, near_pairs), (far_hbm, far_pairs), (rank_hbm, rank_ref)))
    ]
    for copy in copies:
        copy.start()
    heads = head_copies(v_hbm, u_hbm, v_out, u_out, head_sems)
    recv_index, src_index = lax.axis_index("recv"), lax.axis_index("src")
    group_rows = own_clusters * src_count
    source_rows = own_clusters * lax.axis_size("recv")

    def group_place(cluster):
        return ((cluster // group_rows) ^ recv_index) * own_clusters + cluster % own_clusters

    for copy in copies:
        copy.wait()
    tile_count = near_out.shape[0]
    padding = jnp.full((1, lanes - tile_count), -1, jnp.int32)

    def by_device(row):
        return jnp.concatenate(
            [
                jnp.concatenate([near_pairs[row : row + 1, k * tile_count : (k + 1) * tile_count], padding], 1)
                for k in range(src_count)
            ],
            0,
        )

    target, source = by_device(0), by_device(1)
    group = jnp.where(source < 0, -1, (source // own_clusters) % src_count)
    place = jnp.where(source < 0, -1, group_place(source))
    same = [group == g for g in range(src_count)]
    before = lax.broadcasted_iota(jnp.int32, (lanes, lanes), 0) < lax.broadcasted_iota(jnp.int32, (lanes, lanes), 1)
    counts = jnp.dot(
        jnp.concatenate([jnp.where(here, 1.0, 0.0) for here in same], 0).astype(bf16),
        jnp.where(before, 1.0, 0.0).astype(bf16),
        preferred_element_type=f32,
    )
    slot = jnp.zeros(source.shape, f32)
    for g, here in enumerate(same):
        slot += jnp.where(here, counts[g * src_count : (g + 1) * src_count, :], 0.0)
    slot = slot.astype(jnp.int32)
    sent = jnp.where(group == src_index, slot, -1)
    slot_ids = lax.broadcasted_iota(jnp.int32, (capacity, lanes), 0)
    place_ids = lax.broadcasted_iota(jnp.int32, (source_rows, lanes), 0)
    for k in range(src_count):
        from_slot = jnp.where(slot_ids == sent[k : k + 1, :], 1.0, 0.0).astype(bf16)
        from_place = jnp.where(place_ids == place[k : k + 1, :], 1.0, 0.0).astype(bf16)
        pick_out[k * capacity : (k + 1) * capacity, :] = lax.dot_general(
            from_slot, from_place, by_row, preferred_element_type=f32
        ).astype(bf16)
    first_own = recv_index * group_rows + src_index * own_clusters
    code = (target - first_own) * code_base + group * capacity + slot
    own = lax.broadcasted_iota(jnp.int32, code.shape, 0) == src_index
    code = jnp.sum(jnp.where(own, code.astype(f32), 0.0), axis=0, keepdims=True)
    near_out[...] = jnp.transpose(jnp.broadcast_to(code, (lanes, lanes))).astype(jnp.int32)[:tile_count, :]

    per_row = lanes // rank
    group = lanes // per_row
    shape = (group, lanes)
    lane = lax.broadcasted_iota(jnp.int32, shape, 1)
    pick = lax.broadcasted_iota(jnp.int32, shape, 0) * per_row + lane // rank

    def spread(row):
        return jnp.take_along_axis(jnp.broadcast_to(row, shape), pick, axis=1)

    for a in range(rank_ref.shape[0]):
        across = slice(a * lanes, (a + 1) * lanes)
        target = (far_pairs[0:1, across] - recv_index * group_rows) * code_base
        source = spread(target + group_place(far_pairs[1:2, across]))
        missing = spread(target + (code_base - 1))
        far_out[a * group : (a + 1) * group, :] = jnp.where(
            lane % rank < spread(rank_ref[a : a + 1, :]), source, missing
        )
    for copy in heads:
        copy.wait()


def far_part(code_ref, deficit, v_head, u_head, v_buf, u_buf, out_ref, before):
    part = v_buf.shape[0] // chunks
    source_count = deficit.shape[0]
    target_count = out_ref.shape[0]
    source_ids = lax.broadcasted_iota(jnp.int32, (source_count, lanes), 0)
    target_ids = [
        (lax.broadcasted_iota(jnp.int32, (16, lanes), 0) + 16 * k).astype(f32).astype(bf16)
        for k in range(target_count // 16)
    ]
    out_ref[...] = jnp.zeros_like(out_ref)

    step = 0
    for body in bodies:
        base, count = step * part, body * part
        v_ref, u_ref = (v_buf, u_buf) if step else (v_head, u_head)
        if step:
            for i in range(step, step + body):
                before(i)
        products = lax.dot_general(
            deficit, v_ref[base : base + count, :], by_row, preferred_element_type=f32
        )
        spread = []
        for k in range(count // lanes):
            row = base // lanes + k
            code = code_ref[row : row + 1, :]
            source = code % code_base
            target = jnp.broadcast_to((code // code_base).astype(f32), (16, lanes)).astype(bf16)
            coef = jnp.sum(
                jnp.where(source_ids == source, products[:, k * lanes : (k + 1) * lanes], 0.0),
                axis=0,
                keepdims=True,
            )
            coef = jnp.broadcast_to(coef, (16, lanes)).astype(bf16)
            spread.append(
                jnp.concatenate(
                    [jnp.where(ids == target, coef, jnp.zeros_like(coef)) for ids in target_ids], 0
                )
            )
        out_ref[...] += jnp.dot(
            jnp.concatenate(spread, 1), u_ref[base : base + count, :], preferred_element_type=f32
        )
        step += body


def far_kernel(code_ref, pick_ref, *refs):
    parts, (v_head, u_head, v_hbm, u_hbm, out_ref, v_buf, u_buf, sems, total_ref) = refs[:-9], refs[-9:]
    part = v_hbm.shape[0] // chunks

    def copies(i):
        where = slice(i * part, (i + 1) * part)
        return (
            pltpu.make_async_copy(v_hbm.at[where], v_buf.at[where], sems.at[0, i]),
            pltpu.make_async_copy(u_hbm.at[where], u_buf.at[where], sems.at[1, i]),
        )

    for i in range(bodies[0], chunks):
        for copy in copies(i):
            copy.start()

    def before(i):
        for copy in copies(i):
            copy.wait()

    deficit = jnp.concatenate([ref[...] for ref in parts], 0)
    count = parts[0].shape[0]
    picked = jnp.dot(pick_ref[...], deficit, preferred_element_type=f32).astype(bf16)
    capacity = out_ref.shape[1] - count
    for k in range(out_ref.shape[0]):
        out_ref[k, count:, :] = picked[k * capacity : (k + 1) * capacity, :]
    far_part(code_ref, deficit, v_head, u_head, v_buf, u_buf, total_ref, before)
    for k in range(out_ref.shape[0]):
        out_ref[k, :count, :] = total_ref[k * count : (k + 1) * count, :].astype(bf16)


def whole_stress(code_ref, came_ref, tile_ref, count):
    senders = came_ref.shape[0]
    columns = jnp.concatenate([came_ref[k, count:, :] for k in range(senders)], 0)
    tile_count = tile_ref.shape[0]
    code = code_ref[...]
    place, target = code % code_base, code // code_base
    place_ids = lax.broadcasted_iota(jnp.int32, (tile_count, lanes), 1)
    deficits = jnp.zeros((tile_count, lanes), f32)
    for k in range(columns.shape[0] // lanes):
        hot = jnp.where(place_ids + k * lanes == place, 1.0, 0.0).astype(bf16)
        deficits += jnp.dot(hot, columns[k * lanes : (k + 1) * lanes, :], preferred_element_type=f32)
    ids = lax.broadcasted_iota(jnp.int32, (count, lanes), 0)
    placed = [
        jnp.where(ids == target[t : t + 1, :], deficits[t : t + 1, :], 0.0).astype(bf16)
        for t in range(tile_count)
    ]
    near = lax.dot_general(
        jnp.concatenate(placed, 1),
        jnp.concatenate([tile_ref[t] for t in range(tile_count)], 1),
        by_row,
        preferred_element_type=f32,
    )
    far = came_ref[0, :count, :].astype(f32)
    for k in range(1, senders):
        far += came_ref[k, :count, :].astype(f32)
    return far + near


def first_kernel(
    code_ref, came_ref, tile_ref, own_ref, v_hbm, u_hbm, stress_ref, deficit_ref, v_out, u_out, head_sems
):
    heads = head_copies(v_hbm, u_hbm, v_out, u_out, head_sems)
    stress = whole_stress(code_ref, came_ref, tile_ref, stress_ref.shape[0])
    stress_ref[...] = stress
    p, b, plate, theta_rate, gain = [own_ref[k] for k in (0, 3, 5, 6, 7)]
    speed = jnp.exp(p + time_step * ((stress - b * theta_rate) * gain))
    deficit_ref[...] = (plate - speed).astype(bf16)
    for copy in heads:
        copy.wait()


def final_kernel(code_ref, came_ref, tile_ref, own_ref, first_ref, order_ref, p_out, q_out):
    stress = whole_stress(code_ref, came_ref, tile_ref, first_ref.shape[0])
    p, q, a, b, slip, plate, theta_rate, gain = [own_ref[k] for k in range(8)]
    first_p = (first_ref[...] - b * theta_rate) * gain
    speed = jnp.exp(p + time_step * first_p)
    second_q = jnp.exp(-(q + time_step * theta_rate)) - speed / slip
    second_p = (stress - b * second_q) / (a + damping * speed)
    new_p = p + 0.5 * time_step * (first_p + second_p)
    new_q = q + 0.5 * time_step * (theta_rate + second_q)
    pieces = []
    for value in (new_p, new_q):
        for _ in range(3):
            piece = value.astype(bf16).astype(f32)
            value = value - piece
            pieces.append(piece)
    rows = p.shape[0]
    order = order_ref[...]
    row, lane = order // lanes, order % lanes
    row_ids = lax.broadcasted_iota(jnp.int32, (rows, lanes), 0)
    lane_ids = lax.broadcasted_iota(jnp.int32, (lanes, lanes), 0)
    total = jnp.zeros((len(pieces) * rows, lanes), f32)
    for r in range(rows):
        here = row_ids == row[r : r + 1, :]
        placed = jnp.concatenate(
            [jnp.where(here, piece[r : r + 1, :], 0.0) for piece in pieces], 0
        ).astype(bf16)
        spread = jnp.where(lane_ids == lane[r : r + 1, :], 1.0, 0.0).astype(bf16)
        total += lax.dot_general(placed, spread, by_row, preferred_element_type=f32)
    for k, out in enumerate((p_out, q_out)):
        high, mid, low = [total[(3 * k + j) * rows : (3 * k + j + 1) * rows, :] for j in range(3)]
        out[...] = (low + mid) + high


def on_device(
    log_rate,
    log_state,
    a_sigma,
    b_sigma,
    crit_slip,
    plate_rate,
    cluster_order,
    near_tiles,
    near_pairs,
    far_u,
    far_v,
    far_pairs,
    far_ranks,
):
    src_count = lax.axis_size("src")
    recv_count = lax.axis_size("recv")
    device_count = src_count * recv_count
    tile_count = near_tiles.shape[0]
    own_clusters = log_rate.shape[0] // lanes
    group_rows = own_clusters * src_count
    source_rows = own_clusters * recv_count
    far_count, rank = far_u.shape[:2]
    factor_rows = far_count * rank
    params = pltpu.CompilerParams(vmem_limit_bytes=vmem_bytes)
    whole = (own_clusters, lanes)

    arguments = [x.reshape(whole) for x in (log_rate, log_state, a_sigma, b_sigma, crit_slip, plate_rate)]
    own, first_deficit, order = pl.pallas_call(
        order_kernel,
        in_specs=[anywhere] * 7,
        out_specs=(in_vmem,) * 3,
        out_shape=(
            jax.ShapeDtypeStruct((8,) + whole, f32),
            jax.ShapeDtypeStruct(whole, bf16),
            jax.ShapeDtypeStruct(whole, jnp.int32),
        ),
        scratch_shapes=[
            pltpu.VMEM((6,) + whole, f32),
            pltpu.VMEM(whole, jnp.int32),
            pltpu.SemaphoreType.DMA((7,)),
        ],
        compiler_params=params,
    )(*[in_hbm(x) for x in arguments + [cluster_order.reshape(whole)]])

    v_rows = in_hbm(far_v.reshape(factor_rows, lanes))
    u_rows = in_hbm(far_u.reshape(factor_rows, lanes))
    head = jax.ShapeDtypeStruct((factor_rows // chunks * bodies[0], lanes), bf16)
    capacity = -(-max(2, 2 * tile_count // src_count) // 16) * 16
    far_codes, near_codes, picks, *first_heads = pl.pallas_call(
        functools.partial(
            table_kernel, rank=rank, own_clusters=own_clusters, src_count=src_count, capacity=capacity
        ),
        in_specs=[anywhere] * 5,
        out_specs=(in_vmem,) * 5,
        out_shape=(
            jax.ShapeDtypeStruct((factor_rows // lanes, lanes), jnp.int32),
            jax.ShapeDtypeStruct((tile_count, lanes), jnp.int32),
            jax.ShapeDtypeStruct((src_count * capacity, source_rows), bf16),
            head,
            head,
        ),
        scratch_shapes=[
            pltpu.VMEM(near_pairs.shape, jnp.int32),
            pltpu.VMEM(far_pairs.shape, jnp.int32),
            pltpu.VMEM((far_count // lanes, lanes), jnp.int32),
            pltpu.SemaphoreType.DMA((3,)),
            pltpu.SemaphoreType.DMA((2,)),
        ],
        compiler_params=params,
    )(*[in_hbm(x) for x in (near_pairs, far_pairs, far_ranks.reshape(far_count // lanes, lanes))], v_rows, u_rows)

    def exchange(deficit, heads):
        parts = [deficit] + [
            lax.ppermute(deficit, "recv", [(i, i ^ k) for i in range(recv_count)])
            for k in range(1, recv_count)
        ]
        send = pl.pallas_call(
            far_kernel,
            in_specs=[in_vmem] * (4 + recv_count) + [anywhere] * 2,
            out_specs=in_vmem,
            out_shape=jax.ShapeDtypeStruct((src_count, own_clusters + capacity, lanes), bf16),
            scratch_shapes=[
                pltpu.VMEM(v_rows.shape, bf16),
                pltpu.VMEM(u_rows.shape, bf16),
                pltpu.SemaphoreType.DMA((2, chunks)),
                pltpu.VMEM((group_rows, lanes), f32),
            ],
            compiler_params=pltpu.CompilerParams(vmem_limit_bytes=far_vmem_bytes),
            cost_estimate=pl.CostEstimate(
                flops=2 * factor_rows * lanes * (source_rows + group_rows), bytes_accessed=2**24, transcendentals=0
            ),
        )(far_codes, picks, *parts, *heads, v_rows, u_rows)
        return lax.all_to_all(send, "src", split_axis=0, concat_axis=0, tiled=True)

    first_stress, second_deficit, *second_heads = pl.pallas_call(
        first_kernel,
        in_specs=[in_vmem] * 4 + [anywhere] * 2,
        out_specs=(in_vmem,) * 4,
        out_shape=(jax.ShapeDtypeStruct(whole, f32), jax.ShapeDtypeStruct(whole, bf16), head, head),
        scratch_shapes=[pltpu.SemaphoreType.DMA((2,))],
        compiler_params=params,
    )(near_codes, exchange(first_deficit, first_heads), near_tiles, own, v_rows, u_rows)
    new_p, new_q = pl.pallas_call(
        final_kernel,
        out_shape=(jax.ShapeDtypeStruct(whole, f32), jax.ShapeDtypeStruct(whole, f32)),
        compiler_params=params,
    )(near_codes, exchange(second_deficit, second_heads), near_tiles, own, first_stress, order)
    return new_p.reshape(-1), new_q.reshape(-1)


def solution(mesh):
    return jax.shard_map(
        on_device,
        mesh=mesh,
        in_specs=(
            P(("recv", "src")),
            P(("recv", "src")),
            P(("recv", "src")),
            P(("recv", "src")),
            P(("recv", "src")),
            P(("recv", "src")),
            P(("recv", "src"), None),
            P(("recv", "src"), None, None),
            P(None, "recv"),
            P(("recv", "src"), None, None),
            P(("recv", "src"), None, None),
            P(None, ("recv", "src")),
            P(("recv", "src")),
        ),
        out_specs=(P(("recv", "src")), P(("recv", "src"))),
        check_vma=False,
    )
```

```python
import functools

import jax
import jax.numpy as jnp
from jax import lax
from jax.experimental import pallas as pl
from jax.experimental.pallas import tpu as pltpu
from jax.sharding import PartitionSpec as P

time_step = 0.1
damping = 0.5
f32 = jnp.float32
bf16 = jnp.bfloat16
lanes = 128
chunks = 8
code_base = 4096
vmem_bytes = 8 * 2**20
far_vmem_bytes = 28 * 2**20
bodies = (1, 2, 2, 2, 1)
by_row = (((1,), (1,)), ((), ()))
in_vmem = pl.BlockSpec(memory_space=pltpu.VMEM)
anywhere = pl.BlockSpec(memory_space=pl.ANY)


def in_hbm(x):
    return pltpu.with_memory_space_constraint(x, pltpu.HBM)


def gather_rows(arrays, row, lane):
    out = [jnp.zeros(row.shape, f32)] * len(arrays)
    for r in range(row.shape[0]):
        here = row == r
        for k, array in enumerate(arrays):
            spread = jnp.broadcast_to(array[r : r + 1, :], row.shape)
            out[k] = jnp.where(here, jnp.take_along_axis(spread, lane, axis=1), out[k])
    return out


def order_kernel(*refs):
    arguments, (own_ref, deficit_ref, order_out, buf, order_buf, sems) = refs[:7], refs[7:]
    count = len(arguments) - 1
    copies = [
        pltpu.make_async_copy(ref, order_buf if k == count else buf.at[k], sems.at[k])
        for k, ref in enumerate(arguments)
    ]
    for copy in copies:
        copy.start()
    for copy in copies:
        copy.wait()
    order = order_buf[...]
    order_out[...] = order
    row, lane = order // lanes, order % lanes
    p, q, a, b, slip, plate = gather_rows([buf[k] for k in range(count)], row, lane)
    speed = jnp.exp(p)
    theta_rate = jnp.exp(-q) - speed / slip
    gain = 1.0 / (a + damping * speed)
    for k, value in enumerate((p, q, a, b, slip, plate, theta_rate, gain)):
        own_ref[k] = value
    deficit_ref[...] = (plate - speed).astype(bf16)


def head_copies(v_hbm, u_hbm, v_out, u_out, sems):
    copies = [
        pltpu.make_async_copy(there.at[: here.shape[0]], here, sems.at[k])
        for k, (there, here) in enumerate(((v_hbm, v_out), (u_hbm, u_out)))
    ]
    for copy in copies:
        copy.start()
    return copies


def table_kernel(
    near_hbm, far_hbm, rank_hbm, v_hbm, u_hbm, far_out, near_out, pick_out, v_out, u_out,
    near_pairs, far_pairs, rank_ref, sems, head_sems, *,
    rank, own_clusters, src_count, capacity,
):
    copies = [
        pltpu.make_async_copy(there, here, sems.at[k])
        for k, (there, here) in enumerate(((near_hbm, near_pairs), (far_hbm, far_pairs), (rank_hbm, rank_ref)))
    ]
    for copy in copies:
        copy.start()
    heads = head_copies(v_hbm, u_hbm, v_out, u_out, head_sems)
    recv_index, src_index = lax.axis_index("recv"), lax.axis_index("src")
    group_rows = own_clusters * src_count
    source_rows = own_clusters * lax.axis_size("recv")

    def group_place(cluster):
        return ((cluster // group_rows) ^ recv_index) * own_clusters + cluster % own_clusters

    for copy in copies:
        copy.wait()
    tile_count = near_out.shape[0]
    padding = jnp.full((1, lanes - tile_count), -1, jnp.int32)

    def by_device(row):
        return jnp.concatenate(
            [
                jnp.concatenate([near_pairs[row : row + 1, k * tile_count : (k + 1) * tile_count], padding], 1)
                for k in range(src_count)
            ],
            0,
        )

    target, source = by_device(0), by_device(1)
    group = jnp.where(source < 0, -1, (source // own_clusters) % src_count)
    place = jnp.where(source < 0, -1, group_place(source))
    same = [group == g for g in range(src_count)]
    before = lax.broadcasted_iota(jnp.int32, (lanes, lanes), 0) < lax.broadcasted_iota(jnp.int32, (lanes, lanes), 1)
    counts = jnp.dot(
        jnp.concatenate([jnp.where(here, 1.0, 0.0) for here in same], 0).astype(bf16),
        jnp.where(before, 1.0, 0.0).astype(bf16),
        preferred_element_type=f32,
    )
    slot = jnp.zeros(source.shape, f32)
    for g, here in enumerate(same):
        slot += jnp.where(here, counts[g * src_count : (g + 1) * src_count, :], 0.0)
    slot = slot.astype(jnp.int32)
    sent = jnp.where(group == src_index, slot, -1)
    slot_ids = lax.broadcasted_iota(jnp.int32, (capacity, lanes), 0)
    place_ids = lax.broadcasted_iota(jnp.int32, (source_rows, lanes), 0)
    for k in range(src_count):
        from_slot = jnp.where(slot_ids == sent[k : k + 1, :], 1.0, 0.0).astype(bf16)
        from_place = jnp.where(place_ids == place[k : k + 1, :], 1.0, 0.0).astype(bf16)
        pick_out[k * capacity : (k + 1) * capacity, :] = lax.dot_general(
            from_slot, from_place, by_row, preferred_element_type=f32
        ).astype(bf16)
    first_own = recv_index * group_rows + src_index * own_clusters
    code = (target - first_own) * code_base + group * capacity + slot
    own = lax.broadcasted_iota(jnp.int32, code.shape, 0) == src_index
    code = jnp.sum(jnp.where(own, code.astype(f32), 0.0), axis=0, keepdims=True)
    near_out[...] = jnp.transpose(jnp.broadcast_to(code, (lanes, lanes))).astype(jnp.int32)[:tile_count, :]

    per_row = lanes // rank
    group = lanes // per_row
    shape = (group, lanes)
    lane = lax.broadcasted_iota(jnp.int32, shape, 1)
    pick = lax.broadcasted_iota(jnp.int32, shape, 0) * per_row + lane // rank

    def spread(row):
        return jnp.take_along_axis(jnp.broadcast_to(row, shape), pick, axis=1)

    for a in range(rank_ref.shape[0]):
        across = slice(a * lanes, (a + 1) * lanes)
        target = (far_pairs[0:1, across] - recv_index * group_rows) * code_base
        source = spread(target + group_place(far_pairs[1:2, across]))
        missing = spread(target + (code_base - 1))
        far_out[a * group : (a + 1) * group, :] = jnp.where(
            lane % rank < spread(rank_ref[a : a + 1, :]), source, missing
        )
    for copy in heads:
        copy.wait()


def far_part(code_ref, deficit, v_head, u_head, v_buf, u_buf, out_ref, before):
    part = v_buf.shape[0] // chunks
    source_count = deficit.shape[0]
    target_count = out_ref.shape[0]
    source_ids = lax.broadcasted_iota(jnp.int32, (source_count, lanes), 0)
    target_ids = [
        (lax.broadcasted_iota(jnp.int32, (16, lanes), 0) + 16 * k).astype(f32).astype(bf16)
        for k in range(target_count // 16)
    ]
    out_ref[...] = jnp.zeros_like(out_ref)

    step = 0
    for body in bodies:
        base, count = step * part, body * part
        v_ref, u_ref = (v_buf, u_buf) if step else (v_head, u_head)
        if step:
            for i in range(step, step + body):
                before(i)
        products = lax.dot_general(
            deficit, v_ref[base : base + count, :], by_row, preferred_element_type=f32
        )
        spread = []
        for k in range(count // lanes):
            row = base // lanes + k
            code = code_ref[row : row + 1, :]
            source = code % code_base
            target = jnp.broadcast_to((code // code_base).astype(f32), (16, lanes)).astype(bf16)
            coef = jnp.sum(
                jnp.where(source_ids == source, products[:, k * lanes : (k + 1) * lanes], 0.0),
                axis=0,
                keepdims=True,
            )
            coef = jnp.broadcast_to(coef, (16, lanes)).astype(bf16)
            spread.append(
                jnp.concatenate(
                    [jnp.where(ids == target, coef, jnp.zeros_like(coef)) for ids in target_ids], 0
                )
            )
        out_ref[...] += jnp.dot(
            jnp.concatenate(spread, 1), u_ref[base : base + count, :], preferred_element_type=f32
        )
        step += body


def far_kernel(code_ref, pick_ref, *refs):
    parts, (v_head, u_head, v_hbm, u_hbm, out_ref, v_buf, u_buf, sems, total_ref) = refs[:-9], refs[-9:]
    part = v_hbm.shape[0] // chunks

    def copies(i):
        where = slice(i * part, (i + 1) * part)
        return (
            pltpu.make_async_copy(v_hbm.at[where], v_buf.at[where], sems.at[0, i]),
            pltpu.make_async_copy(u_hbm.at[where], u_buf.at[where], sems.at[1, i]),
        )

    for i in range(bodies[0], chunks):
        for copy in copies(i):
            copy.start()

    def before(i):
        for copy in copies(i):
            copy.wait()

    deficit = jnp.concatenate([ref[...] for ref in parts], 0)
    count = parts[0].shape[0]
    picked = jnp.dot(pick_ref[...], deficit, preferred_element_type=f32).astype(bf16)
    capacity = out_ref.shape[1] - count
    for k in range(out_ref.shape[0]):
        out_ref[k, count:, :] = picked[k * capacity : (k + 1) * capacity, :]
    far_part(code_ref, deficit, v_head, u_head, v_buf, u_buf, total_ref, before)
    for k in range(out_ref.shape[0]):
        out_ref[k, :count, :] = total_ref[k * count : (k + 1) * count, :].astype(bf16)


def whole_stress(code_ref, came_ref, tile_ref, count):
    senders = came_ref.shape[0]
    columns = jnp.concatenate([came_ref[k, count:, :] for k in range(senders)], 0)
    tile_count = tile_ref.shape[0]
    code = code_ref[...]
    place, target = code % code_base, code // code_base
    place_ids = lax.broadcasted_iota(jnp.int32, (tile_count, lanes), 1)
    deficits = jnp.zeros((tile_count, lanes), f32)
    for k in range(columns.shape[0] // lanes):
        hot = jnp.where(place_ids + k * lanes == place, 1.0, 0.0).astype(bf16)
        deficits += jnp.dot(hot, columns[k * lanes : (k + 1) * lanes, :], preferred_element_type=f32)
    ids = lax.broadcasted_iota(jnp.int32, (count, lanes), 0)
    placed = [
        jnp.where(ids == target[t : t + 1, :], deficits[t : t + 1, :], 0.0).astype(bf16)
        for t in range(tile_count)
    ]
    near = lax.dot_general(
        jnp.concatenate(placed, 1),
        jnp.concatenate([tile_ref[t] for t in range(tile_count)], 1),
        by_row,
        preferred_element_type=f32,
    )
    far = came_ref[0, :count, :].astype(f32)
    for k in range(1, senders):
        far += came_ref[k, :count, :].astype(f32)
    return far + near


def first_kernel(code_ref, came_ref, tile_ref, own_ref, stress_ref, deficit_ref):
    stress = whole_stress(code_ref, came_ref, tile_ref, stress_ref.shape[0])
    stress_ref[...] = stress
    p, b, plate, theta_rate, gain = [own_ref[k] for k in (0, 3, 5, 6, 7)]
    speed = jnp.exp(p + time_step * ((stress - b * theta_rate) * gain))
    deficit_ref[...] = (plate - speed).astype(bf16)


def ahead_kernel(own_ref, first_ref, order_ref, v_hbm, u_hbm, keep_ref, back_ref, q_out, v_out, u_out, head_sems):
    heads = head_copies(v_hbm, u_hbm, v_out, u_out, head_sems)
    order = order_ref[...]
    rows = order.shape[0]
    row, lane = order // lanes, order % lanes
    row_ids = lax.broadcasted_iota(jnp.int32, (rows, lanes), 0)
    position = lax.broadcasted_iota(jnp.int32, (rows, lanes), 1).astype(f32)
    lane_ids = lax.broadcasted_iota(jnp.int32, (lanes, lanes), 0)
    total = jnp.zeros((2 * rows, lanes), f32)
    for r in range(rows):
        here = row_ids == row[r : r + 1, :]
        placed = jnp.concatenate([jnp.where(here, float(r), 0.0), jnp.where(here, position, 0.0)], 0)
        spread = jnp.where(lane_ids == lane[r : r + 1, :], 1.0, 0.0).astype(bf16)
        total += lax.dot_general(placed.astype(bf16), spread, by_row, preferred_element_type=f32)
    back_row, back_lane = total[:rows].astype(jnp.int32), total[rows:].astype(jnp.int32)
    back_ref[0] = back_row
    back_ref[1] = back_lane

    p, q, a, b, slip, plate, theta_rate, gain = [own_ref[k] for k in range(8)]
    first_p = (first_ref[...] - b * theta_rate) * gain
    speed = jnp.exp(p + time_step * first_p)
    second_q = jnp.exp(-(q + time_step * theta_rate)) - speed / slip
    second_gain = 0.5 * time_step / (a + damping * speed)
    new_q, offset, factor = gather_rows(
        (
            q + 0.5 * time_step * (theta_rate + second_q),
            p + 0.5 * time_step * first_p - b * second_q * second_gain,
            second_gain,
        ),
        back_row,
        back_lane,
    )
    q_out[...] = new_q
    keep_ref[0] = offset
    keep_ref[1] = factor
    for copy in heads:
        copy.wait()


def final_kernel(code_ref, came_ref, tile_ref, keep_ref, back_ref, p_out):
    stress = whole_stress(code_ref, came_ref, tile_ref, p_out.shape[0])
    (stress,) = gather_rows((stress,), back_ref[0], back_ref[1])
    p_out[...] = keep_ref[0] + keep_ref[1] * stress


def on_device(
    log_rate,
    log_state,
    a_sigma,
    b_sigma,
    crit_slip,
    plate_rate,
    cluster_order,
    near_tiles,
    near_pairs,
    far_u,
    far_v,
    far_pairs,
    far_ranks,
):
    src_count = lax.axis_size("src")
    recv_count = lax.axis_size("recv")
    device_count = src_count * recv_count
    tile_count = near_tiles.shape[0]
    own_clusters = log_rate.shape[0] // lanes
    group_rows = own_clusters * src_count
    source_rows = own_clusters * recv_count
    far_count, rank = far_u.shape[:2]
    factor_rows = far_count * rank
    params = pltpu.CompilerParams(vmem_limit_bytes=vmem_bytes)
    whole = (own_clusters, lanes)

    arguments = [x.reshape(whole) for x in (log_rate, log_state, a_sigma, b_sigma, crit_slip, plate_rate)]
    own, first_deficit, order = pl.pallas_call(
        order_kernel,
        in_specs=[anywhere] * 7,
        out_specs=(in_vmem,) * 3,
        out_shape=(
            jax.ShapeDtypeStruct((8,) + whole, f32),
            jax.ShapeDtypeStruct(whole, bf16),
            jax.ShapeDtypeStruct(whole, jnp.int32),
        ),
        scratch_shapes=[
            pltpu.VMEM((6,) + whole, f32),
            pltpu.VMEM(whole, jnp.int32),
            pltpu.SemaphoreType.DMA((7,)),
        ],
        compiler_params=params,
    )(*[in_hbm(x) for x in arguments + [cluster_order.reshape(whole)]])

    v_rows = in_hbm(far_v.reshape(factor_rows, lanes))
    u_rows = in_hbm(far_u.reshape(factor_rows, lanes))
    head = jax.ShapeDtypeStruct((factor_rows // chunks * bodies[0], lanes), bf16)
    capacity = -(-max(2, 2 * tile_count // src_count) // 16) * 16
    far_codes, near_codes, picks, *first_heads = pl.pallas_call(
        functools.partial(
            table_kernel, rank=rank, own_clusters=own_clusters, src_count=src_count, capacity=capacity
        ),
        in_specs=[anywhere] * 5,
        out_specs=(in_vmem,) * 5,
        out_shape=(
            jax.ShapeDtypeStruct((factor_rows // lanes, lanes), jnp.int32),
            jax.ShapeDtypeStruct((tile_count, lanes), jnp.int32),
            jax.ShapeDtypeStruct((src_count * capacity, source_rows), bf16),
            head,
            head,
        ),
        scratch_shapes=[
            pltpu.VMEM(near_pairs.shape, jnp.int32),
            pltpu.VMEM(far_pairs.shape, jnp.int32),
            pltpu.VMEM((far_count // lanes, lanes), jnp.int32),
            pltpu.SemaphoreType.DMA((3,)),
            pltpu.SemaphoreType.DMA((2,)),
        ],
        compiler_params=params,
    )(*[in_hbm(x) for x in (near_pairs, far_pairs, far_ranks.reshape(far_count // lanes, lanes))], v_rows, u_rows)

    def exchange(deficit, heads):
        parts = [deficit] + [
            lax.ppermute(deficit, "recv", [(i, i ^ k) for i in range(recv_count)])
            for k in range(1, recv_count)
        ]
        send = pl.pallas_call(
            far_kernel,
            in_specs=[in_vmem] * (4 + recv_count) + [anywhere] * 2,
            out_specs=in_vmem,
            out_shape=jax.ShapeDtypeStruct((src_count, own_clusters + capacity, lanes), bf16),
            scratch_shapes=[
                pltpu.VMEM(v_rows.shape, bf16),
                pltpu.VMEM(u_rows.shape, bf16),
                pltpu.SemaphoreType.DMA((2, chunks)),
                pltpu.VMEM((group_rows, lanes), f32),
            ],
            compiler_params=pltpu.CompilerParams(vmem_limit_bytes=far_vmem_bytes),
            cost_estimate=pl.CostEstimate(
                flops=2 * factor_rows * lanes * (source_rows + group_rows), bytes_accessed=2**24, transcendentals=0
            ),
        )(far_codes, picks, *parts, *heads, v_rows, u_rows)
        return lax.all_to_all(send, "src", split_axis=0, concat_axis=0, tiled=True)

    state = jax.ShapeDtypeStruct(whole, f32)
    first_stress, second_deficit = pl.pallas_call(
        first_kernel,
        in_specs=[in_vmem] * 4,
        out_specs=(in_vmem,) * 2,
        out_shape=(state, jax.ShapeDtypeStruct(whole, bf16)),
        compiler_params=params,
    )(near_codes, exchange(first_deficit, first_heads), near_tiles, own)
    keep, back, new_q, *second_heads = pl.pallas_call(
        ahead_kernel,
        in_specs=[in_vmem] * 3 + [anywhere] * 2,
        out_specs=(in_vmem,) * 5,
        out_shape=(
            jax.ShapeDtypeStruct((2,) + whole, f32),
            jax.ShapeDtypeStruct((2,) + whole, jnp.int32),
            state,
            head,
            head,
        ),
        scratch_shapes=[pltpu.SemaphoreType.DMA((2,))],
        compiler_params=params,
    )(own, first_stress, order, v_rows, u_rows)
    new_p = pl.pallas_call(
        final_kernel,
        in_specs=[in_vmem] * 5,
        out_specs=in_vmem,
        out_shape=state,
        compiler_params=params,
    )(near_codes, exchange(second_deficit, second_heads), near_tiles, keep, back)
    return new_p.reshape(-1), new_q.reshape(-1)


def solution(mesh):
    return jax.shard_map(
        on_device,
        mesh=mesh,
        in_specs=(
            P(("recv", "src")),
            P(("recv", "src")),
            P(("recv", "src")),
            P(("recv", "src")),
            P(("recv", "src")),
            P(("recv", "src")),
            P(("recv", "src"), None),
            P(("recv", "src"), None, None),
            P(None, "recv"),
            P(("recv", "src"), None, None),
            P(("recv", "src"), None, None),
            P(None, ("recv", "src")),
            P(("recv", "src")),
        ),
        out_specs=(P(("recv", "src")), P(("recv", "src"))),
        check_vma=False,
    )
```

```python
import functools

import jax
import jax.numpy as jnp
from jax import lax
from jax.experimental import pallas as pl
from jax.experimental.pallas import tpu as pltpu
from jax.sharding import PartitionSpec as P

time_step = 0.1
damping = 0.5
f32 = jnp.float32
bf16 = jnp.bfloat16
lanes = 128
chunks = 8
code_base = 4096
vmem_bytes = 16 * 2**20
far_vmem_bytes = 40 * 2**20
bodies = (3, 2, 2, 1)
by_row = (((1,), (1,)), ((), ()))
in_vmem = pl.BlockSpec(memory_space=pltpu.VMEM)
anywhere = pl.BlockSpec(memory_space=pl.ANY)


def in_hbm(x):
    return pltpu.with_memory_space_constraint(x, pltpu.HBM)


def gather_rows(arrays, row, lane):
    out = [jnp.zeros(row.shape, f32)] * len(arrays)
    for r in range(row.shape[0]):
        here = row == r
        for k, array in enumerate(arrays):
            spread = jnp.broadcast_to(array[r : r + 1, :], row.shape)
            out[k] = jnp.where(here, jnp.take_along_axis(spread, lane, axis=1), out[k])
    return out


def order_kernel(*refs):
    arguments, (own_ref, deficit_ref, order_out, buf, order_buf, sems) = refs[:7], refs[7:]
    count = len(arguments) - 1
    copies = [
        pltpu.make_async_copy(ref, order_buf if k == count else buf.at[k], sems.at[k])
        for k, ref in enumerate(arguments)
    ]
    for copy in copies:
        copy.start()
    for copy in copies:
        copy.wait()
    order = order_buf[...]
    order_out[...] = order
    row, lane = order // lanes, order % lanes
    p, q, a, b, slip, plate = gather_rows([buf[k] for k in range(count)], row, lane)
    speed = jnp.exp(p)
    theta_rate = jnp.exp(-q) - speed / slip
    gain = 1.0 / (a + damping * speed)
    for k, value in enumerate((p, q, a, b, slip, plate, theta_rate, gain)):
        own_ref[k] = value
    deficit_ref[...] = (plate - speed).astype(bf16)


def head_copies(v_hbm, u_hbm, v_out, u_out, sems):
    copies = [
        pltpu.make_async_copy(there.at[: here.shape[0]], here, sems.at[k])
        for k, (there, here) in enumerate(((v_hbm, v_out), (u_hbm, u_out)))
    ]
    for copy in copies:
        copy.start()
    return copies


def table_kernel(
    near_hbm, far_hbm, rank_hbm, v_hbm, u_hbm, far_out, near_out, pick_out, v_out, u_out,
    near_pairs, far_pairs, rank_ref, sems, head_sems, *,
    rank, own_clusters, src_count, capacity,
):
    copies = [
        pltpu.make_async_copy(there, here, sems.at[k])
        for k, (there, here) in enumerate(((near_hbm, near_pairs), (far_hbm, far_pairs), (rank_hbm, rank_ref)))
    ]
    for copy in copies:
        copy.start()
    heads = head_copies(v_hbm, u_hbm, v_out, u_out, head_sems)
    recv_index, src_index = lax.axis_index("recv"), lax.axis_index("src")
    group_rows = own_clusters * src_count
    source_rows = own_clusters * lax.axis_size("recv")

    def group_place(cluster):
        return ((cluster // group_rows) ^ recv_index) * own_clusters + cluster % own_clusters

    for copy in copies:
        copy.wait()
    tile_count = near_out.shape[0]
    padding = jnp.full((1, lanes - tile_count), -1, jnp.int32)

    def by_device(row):
        return jnp.concatenate(
            [
                jnp.concatenate([near_pairs[row : row + 1, k * tile_count : (k + 1) * tile_count], padding], 1)
                for k in range(src_count)
            ],
            0,
        )

    target, source = by_device(0), by_device(1)
    group = jnp.where(source < 0, -1, (source // own_clusters) % src_count)
    place = jnp.where(source < 0, -1, group_place(source))
    same = [group == g for g in range(src_count)]
    before = lax.broadcasted_iota(jnp.int32, (lanes, lanes), 0) < lax.broadcasted_iota(jnp.int32, (lanes, lanes), 1)
    counts = jnp.dot(
        jnp.concatenate([jnp.where(here, 1.0, 0.0) for here in same], 0).astype(bf16),
        jnp.where(before, 1.0, 0.0).astype(bf16),
        preferred_element_type=f32,
    )
    slot = jnp.zeros(source.shape, f32)
    for g, here in enumerate(same):
        slot += jnp.where(here, counts[g * src_count : (g + 1) * src_count, :], 0.0)
    slot = slot.astype(jnp.int32)
    sent = jnp.where(group == src_index, slot, -1)
    slot_ids = lax.broadcasted_iota(jnp.int32, (capacity, lanes), 0)
    place_ids = lax.broadcasted_iota(jnp.int32, (source_rows, lanes), 0)
    for k in range(src_count):
        from_slot = jnp.where(slot_ids == sent[k : k + 1, :], 1.0, 0.0).astype(bf16)
        from_place = jnp.where(place_ids == place[k : k + 1, :], 1.0, 0.0).astype(bf16)
        pick_out[k * capacity : (k + 1) * capacity, :] = lax.dot_general(
            from_slot, from_place, by_row, preferred_element_type=f32
        ).astype(bf16)
    first_own = recv_index * group_rows + src_index * own_clusters
    code = (target - first_own) * code_base + group * capacity + slot
    own = lax.broadcasted_iota(jnp.int32, code.shape, 0) == src_index
    code = jnp.sum(jnp.where(own, code.astype(f32), 0.0), axis=0, keepdims=True)
    near_out[...] = jnp.transpose(jnp.broadcast_to(code, (lanes, lanes))).astype(jnp.int32)[:tile_count, :]

    per_row = lanes // rank
    group = lanes // per_row
    shape = (group, lanes)
    lane = lax.broadcasted_iota(jnp.int32, shape, 1)
    pick = lax.broadcasted_iota(jnp.int32, shape, 0) * per_row + lane // rank

    def spread(row):
        return jnp.take_along_axis(jnp.broadcast_to(row, shape), pick, axis=1)

    for a in range(rank_ref.shape[0]):
        across = slice(a * lanes, (a + 1) * lanes)
        target = (far_pairs[0:1, across] - recv_index * group_rows) * code_base
        source = spread(target + group_place(far_pairs[1:2, across]))
        missing = spread(target + (code_base - 1))
        far_out[a * group : (a + 1) * group, :] = jnp.where(
            lane % rank < spread(rank_ref[a : a + 1, :]), source, missing
        )
    for copy in heads:
        copy.wait()


def far_part(code_ref, deficit, v_head, u_head, v_buf, u_buf, out_ref, before):
    part = v_buf.shape[0] // chunks
    source_count = deficit.shape[0]
    target_count = out_ref.shape[0]
    source_ids = lax.broadcasted_iota(jnp.int32, (source_count, lanes), 0)
    target_ids = [
        (lax.broadcasted_iota(jnp.int32, (16, lanes), 0) + 16 * k).astype(f32).astype(bf16)
        for k in range(target_count // 16)
    ]
    out_ref[...] = jnp.zeros_like(out_ref)

    step = 0
    for body in bodies:
        base, count = step * part, body * part
        v_ref, u_ref = (v_buf, u_buf) if step else (v_head, u_head)
        if step:
            for i in range(step, step + body):
                before(i)
        products = lax.dot_general(
            deficit, v_ref[base : base + count, :], by_row, preferred_element_type=f32
        )
        spread = []
        for k in range(count // lanes):
            row = base // lanes + k
            code = code_ref[row : row + 1, :]
            source = code % code_base
            target = jnp.broadcast_to((code // code_base).astype(f32), (16, lanes)).astype(bf16)
            coef = jnp.sum(
                jnp.where(source_ids == source, products[:, k * lanes : (k + 1) * lanes], 0.0),
                axis=0,
                keepdims=True,
            )
            coef = jnp.broadcast_to(coef, (16, lanes)).astype(bf16)
            spread.append(
                jnp.concatenate(
                    [jnp.where(ids == target, coef, jnp.zeros_like(coef)) for ids in target_ids], 0
                )
            )
        out_ref[...] += jnp.dot(
            jnp.concatenate(spread, 1), u_ref[base : base + count, :], preferred_element_type=f32
        )
        step += body


def far_kernel(code_ref, pick_ref, *refs):
    parts, (v_head, u_head, v_hbm, u_hbm, out_ref, v_buf, u_buf, sems, total_ref) = refs[:-9], refs[-9:]
    part = v_hbm.shape[0] // chunks

    def copies(i):
        where = slice(i * part, (i + 1) * part)
        return (
            pltpu.make_async_copy(v_hbm.at[where], v_buf.at[where], sems.at[0, i]),
            pltpu.make_async_copy(u_hbm.at[where], u_buf.at[where], sems.at[1, i]),
        )

    for i in range(bodies[0], chunks):
        for copy in copies(i):
            copy.start()

    def before(i):
        for copy in copies(i):
            copy.wait()

    deficit = jnp.concatenate([ref[...] for ref in parts], 0)
    count = parts[0].shape[0]
    picked = jnp.dot(pick_ref[...], deficit, preferred_element_type=f32).astype(bf16)
    capacity = out_ref.shape[1] - count
    for k in range(out_ref.shape[0]):
        out_ref[k, count:, :] = picked[k * capacity : (k + 1) * capacity, :]
    far_part(code_ref, deficit, v_head, u_head, v_buf, u_buf, total_ref, before)
    for k in range(out_ref.shape[0]):
        out_ref[k, :count, :] = total_ref[k * count : (k + 1) * count, :].astype(bf16)


def whole_stress(code_ref, came_ref, tile_ref, count):
    senders = came_ref.shape[0]
    columns = jnp.concatenate([came_ref[k, count:, :] for k in range(senders)], 0)
    tile_count = tile_ref.shape[0]
    code = code_ref[...]
    place, target = code % code_base, code // code_base
    place_ids = lax.broadcasted_iota(jnp.int32, (tile_count, lanes), 1)
    deficits = jnp.zeros((tile_count, lanes), f32)
    for k in range(columns.shape[0] // lanes):
        hot = jnp.where(place_ids + k * lanes == place, 1.0, 0.0).astype(bf16)
        deficits += jnp.dot(hot, columns[k * lanes : (k + 1) * lanes, :], preferred_element_type=f32)
    ids = lax.broadcasted_iota(jnp.int32, (count, lanes), 0)
    placed = [
        jnp.where(ids == target[t : t + 1, :], deficits[t : t + 1, :], 0.0).astype(bf16)
        for t in range(tile_count)
    ]
    near = lax.dot_general(
        jnp.concatenate(placed, 1),
        jnp.concatenate([tile_ref[t] for t in range(tile_count)], 1),
        by_row,
        preferred_element_type=f32,
    )
    far = came_ref[0, :count, :].astype(f32)
    for k in range(1, senders):
        far += came_ref[k, :count, :].astype(f32)
    return far + near


def first_kernel(code_ref, came_ref, tile_ref, own_ref, stress_ref, deficit_ref):
    stress = whole_stress(code_ref, came_ref, tile_ref, stress_ref.shape[0])
    stress_ref[...] = stress
    p, b, plate, theta_rate, gain = [own_ref[k] for k in (0, 3, 5, 6, 7)]
    speed = jnp.exp(p + time_step * ((stress - b * theta_rate) * gain))
    deficit_ref[...] = (plate - speed).astype(bf16)


def ahead_kernel(own_ref, first_ref, order_ref, v_hbm, u_hbm, keep_ref, back_ref, q_out, v_out, u_out, head_sems):
    heads = head_copies(v_hbm, u_hbm, v_out, u_out, head_sems)
    order = order_ref[...]
    rows = order.shape[0]
    row, lane = order // lanes, order % lanes
    row_ids = lax.broadcasted_iota(jnp.int32, (rows, lanes), 0)
    position = lax.broadcasted_iota(jnp.int32, (rows, lanes), 1).astype(f32)
    lane_ids = lax.broadcasted_iota(jnp.int32, (lanes, lanes), 0)
    placed, spread = [], []
    for r in range(rows):
        here = row_ids == row[r : r + 1, :]
        placed.append(jnp.concatenate([jnp.where(here, float(r), 0.0), jnp.where(here, position, 0.0)], 0).astype(bf16))
        spread.append(jnp.where(lane_ids == lane[r : r + 1, :], 1.0, 0.0).astype(bf16))
    total = lax.dot_general(
        jnp.concatenate(placed, 1), jnp.concatenate(spread, 1), by_row, preferred_element_type=f32
    )
    back_row, back_lane = total[:rows].astype(jnp.int32), total[rows:].astype(jnp.int32)
    back_ref[0] = back_row
    back_ref[1] = back_lane

    p, q, a, b, slip, plate, theta_rate, gain = [own_ref[k] for k in range(8)]
    first_p = (first_ref[...] - b * theta_rate) * gain
    speed = jnp.exp(p + time_step * first_p)
    second_q = jnp.exp(-(q + time_step * theta_rate)) - speed / slip
    second_gain = 0.5 * time_step / (a + damping * speed)
    new_q, offset, factor = gather_rows(
        (
            q + 0.5 * time_step * (theta_rate + second_q),
            p + 0.5 * time_step * first_p - b * second_q * second_gain,
            second_gain,
        ),
        back_row,
        back_lane,
    )
    q_out[...] = new_q
    keep_ref[0] = offset
    keep_ref[1] = factor
    for copy in heads:
        copy.wait()


def final_kernel(code_ref, came_ref, tile_ref, keep_ref, back_ref, p_out):
    stress = whole_stress(code_ref, came_ref, tile_ref, p_out.shape[0])
    (stress,) = gather_rows((stress,), back_ref[0], back_ref[1])
    p_out[...] = keep_ref[0] + keep_ref[1] * stress


def on_device(
    log_rate,
    log_state,
    a_sigma,
    b_sigma,
    crit_slip,
    plate_rate,
    cluster_order,
    near_tiles,
    near_pairs,
    far_u,
    far_v,
    far_pairs,
    far_ranks,
):
    src_count = lax.axis_size("src")
    recv_count = lax.axis_size("recv")
    device_count = src_count * recv_count
    tile_count = near_tiles.shape[0]
    own_clusters = log_rate.shape[0] // lanes
    group_rows = own_clusters * src_count
    source_rows = own_clusters * recv_count
    far_count, rank = far_u.shape[:2]
    factor_rows = far_count * rank
    params = pltpu.CompilerParams(vmem_limit_bytes=vmem_bytes)
    whole = (own_clusters, lanes)

    arguments = [x.reshape(whole) for x in (log_rate, log_state, a_sigma, b_sigma, crit_slip, plate_rate)]
    own, first_deficit, order = pl.pallas_call(
        order_kernel,
        in_specs=[anywhere] * 7,
        out_specs=(in_vmem,) * 3,
        out_shape=(
            jax.ShapeDtypeStruct((8,) + whole, f32),
            jax.ShapeDtypeStruct(whole, bf16),
            jax.ShapeDtypeStruct(whole, jnp.int32),
        ),
        scratch_shapes=[
            pltpu.VMEM((6,) + whole, f32),
            pltpu.VMEM(whole, jnp.int32),
            pltpu.SemaphoreType.DMA((7,)),
        ],
        compiler_params=params,
    )(*[in_hbm(x) for x in arguments + [cluster_order.reshape(whole)]])

    v_rows = in_hbm(far_v.reshape(factor_rows, lanes))
    u_rows = in_hbm(far_u.reshape(factor_rows, lanes))
    head = jax.ShapeDtypeStruct((factor_rows // chunks * bodies[0], lanes), bf16)
    capacity = -(-max(2, 2 * tile_count // src_count) // 16) * 16
    far_codes, near_codes, picks, *first_heads = pl.pallas_call(
        functools.partial(
            table_kernel, rank=rank, own_clusters=own_clusters, src_count=src_count, capacity=capacity
        ),
        in_specs=[anywhere] * 5,
        out_specs=(in_vmem,) * 5,
        out_shape=(
            jax.ShapeDtypeStruct((factor_rows // lanes, lanes), jnp.int32),
            jax.ShapeDtypeStruct((tile_count, lanes), jnp.int32),
            jax.ShapeDtypeStruct((src_count * capacity, source_rows), bf16),
            head,
            head,
        ),
        scratch_shapes=[
            pltpu.VMEM(near_pairs.shape, jnp.int32),
            pltpu.VMEM(far_pairs.shape, jnp.int32),
            pltpu.VMEM((far_count // lanes, lanes), jnp.int32),
            pltpu.SemaphoreType.DMA((3,)),
            pltpu.SemaphoreType.DMA((2,)),
        ],
        compiler_params=params,
    )(*[in_hbm(x) for x in (near_pairs, far_pairs, far_ranks.reshape(far_count // lanes, lanes))], v_rows, u_rows)

    def exchange(deficit, heads):
        parts = [deficit] + [
            lax.ppermute(deficit, "recv", [(i, i ^ k) for i in range(recv_count)])
            for k in range(1, recv_count)
        ]
        send = pl.pallas_call(
            far_kernel,
            in_specs=[in_vmem] * (4 + recv_count) + [anywhere] * 2,
            out_specs=in_vmem,
            out_shape=jax.ShapeDtypeStruct((src_count, own_clusters + capacity, lanes), bf16),
            scratch_shapes=[
                pltpu.VMEM(v_rows.shape, bf16),
                pltpu.VMEM(u_rows.shape, bf16),
                pltpu.SemaphoreType.DMA((2, chunks)),
                pltpu.VMEM((group_rows, lanes), f32),
            ],
            compiler_params=pltpu.CompilerParams(vmem_limit_bytes=far_vmem_bytes),
            cost_estimate=pl.CostEstimate(
                flops=2 * factor_rows * lanes * (source_rows + group_rows), bytes_accessed=2**24, transcendentals=0
            ),
        )(far_codes, picks, *parts, *heads, v_rows, u_rows)
        return lax.all_to_all(send, "src", split_axis=0, concat_axis=0, tiled=True)

    state = jax.ShapeDtypeStruct(whole, f32)
    first_stress, second_deficit = pl.pallas_call(
        first_kernel,
        in_specs=[in_vmem] * 4,
        out_specs=(in_vmem,) * 2,
        out_shape=(state, jax.ShapeDtypeStruct(whole, bf16)),
        compiler_params=params,
    )(near_codes, exchange(first_deficit, first_heads), near_tiles, own)
    keep, back, new_q, *second_heads = pl.pallas_call(
        ahead_kernel,
        in_specs=[in_vmem] * 3 + [anywhere] * 2,
        out_specs=(in_vmem,) * 5,
        out_shape=(
            jax.ShapeDtypeStruct((2,) + whole, f32),
            jax.ShapeDtypeStruct((2,) + whole, jnp.int32),
            state,
            head,
            head,
        ),
        scratch_shapes=[pltpu.SemaphoreType.DMA((2,))],
        compiler_params=params,
    )(own, first_stress, order, v_rows, u_rows)
    new_p = pl.pallas_call(
        final_kernel,
        in_specs=[in_vmem] * 5,
        out_specs=in_vmem,
        out_shape=state,
        compiler_params=params,
    )(near_codes, exchange(second_deficit, second_heads), near_tiles, keep, back)
    return new_p.reshape(-1), new_q.reshape(-1)


def solution(mesh):
    return jax.shard_map(
        on_device,
        mesh=mesh,
        in_specs=(
            P(("recv", "src")),
            P(("recv", "src")),
            P(("recv", "src")),
            P(("recv", "src")),
            P(("recv", "src")),
            P(("recv", "src")),
            P(("recv", "src"), None),
            P(("recv", "src"), None, None),
            P(None, "recv"),
            P(("recv", "src"), None, None),
            P(("recv", "src"), None, None),
            P(None, ("recv", "src")),
            P(("recv", "src")),
        ),
        out_specs=(P(("recv", "src")), P(("recv", "src"))),
        check_vma=False,
    )
```

```python
import functools

import jax
import jax.numpy as jnp
from jax import lax
from jax.experimental import pallas as pl
from jax.experimental.pallas import tpu as pltpu
from jax.sharding import PartitionSpec as P

time_step = 0.1
damping = 0.5
f32 = jnp.float32
bf16 = jnp.bfloat16
lanes = 128
chunks = 8
code_base = 4096
vmem_bytes = 16 * 2**20
far_vmem_bytes = 40 * 2**20
bodies = (3, 2, 2, 1)
by_row = (((1,), (1,)), ((), ()))
in_vmem = pl.BlockSpec(memory_space=pltpu.VMEM)
anywhere = pl.BlockSpec(memory_space=pl.ANY)


def in_hbm(x):
    return pltpu.with_memory_space_constraint(x, pltpu.HBM)


def gather_rows(arrays, row, lane):
    out = [jnp.zeros(row.shape, f32)] * len(arrays)
    for r in range(row.shape[0]):
        here = row == r
        for k, array in enumerate(arrays):
            spread = jnp.broadcast_to(array[r : r + 1, :], row.shape)
            out[k] = jnp.where(here, jnp.take_along_axis(spread, lane, axis=1), out[k])
    return out


def order_kernel(p_hbm, plate_hbm, order_hbm, own_ref, deficit_ref, order_ref, buf, sems):
    copies = [
        pltpu.make_async_copy(there, here, sems.at[k])
        for k, (there, here) in enumerate(((p_hbm, buf.at[0]), (plate_hbm, buf.at[1]), (order_hbm, order_ref)))
    ]
    for copy in copies:
        copy.start()
    for copy in copies:
        copy.wait()
    order = order_ref[...]
    p, plate = gather_rows((buf[0], buf[1]), order // lanes, order % lanes)
    own_ref[0] = p
    own_ref[1] = plate
    deficit_ref[...] = (plate - jnp.exp(p)).astype(bf16)


def head_copies(v_hbm, u_hbm, v_out, u_out, sems):
    copies = [
        pltpu.make_async_copy(there.at[: here.shape[0]], here, sems.at[k])
        for k, (there, here) in enumerate(((v_hbm, v_out), (u_hbm, u_out)))
    ]
    for copy in copies:
        copy.start()
    return copies


def table_kernel(
    near_hbm, far_hbm, rank_hbm, q_hbm, a_hbm, b_hbm, slip_hbm, v_hbm, u_hbm, mine_ref, order_ref,
    far_out, near_out, pick_out, own_out, v_out, u_out,
    near_pairs, far_pairs, rank_ref, buf, sems, head_sems, *,
    rank, own_clusters, src_count, capacity,
):
    ends = [(near_hbm, near_pairs), (far_hbm, far_pairs), (rank_hbm, rank_ref)]
    ends += [(there, buf.at[k]) for k, there in enumerate((q_hbm, a_hbm, b_hbm, slip_hbm))]
    copies = [pltpu.make_async_copy(there, here, sems.at[k]) for k, (there, here) in enumerate(ends)]
    for copy in copies:
        copy.start()
    heads = head_copies(v_hbm, u_hbm, v_out, u_out, head_sems)
    recv_index, src_index = lax.axis_index("recv"), lax.axis_index("src")
    group_rows = own_clusters * src_count
    source_rows = own_clusters * lax.axis_size("recv")

    def group_place(cluster):
        return ((cluster // group_rows) ^ recv_index) * own_clusters + cluster % own_clusters

    for copy in copies:
        copy.wait()
    tile_count = near_out.shape[0]
    padding = jnp.full((1, lanes - tile_count), -1, jnp.int32)

    def by_device(row):
        return jnp.concatenate(
            [
                jnp.concatenate([near_pairs[row : row + 1, k * tile_count : (k + 1) * tile_count], padding], 1)
                for k in range(src_count)
            ],
            0,
        )

    target, source = by_device(0), by_device(1)
    group = jnp.where(source < 0, -1, (source // own_clusters) % src_count)
    place = jnp.where(source < 0, -1, group_place(source))
    same = [group == g for g in range(src_count)]
    before = lax.broadcasted_iota(jnp.int32, (lanes, lanes), 0) < lax.broadcasted_iota(jnp.int32, (lanes, lanes), 1)
    counts = jnp.dot(
        jnp.concatenate([jnp.where(here, 1.0, 0.0) for here in same], 0).astype(bf16),
        jnp.where(before, 1.0, 0.0).astype(bf16),
        preferred_element_type=f32,
    )
    slot = jnp.zeros(source.shape, f32)
    for g, here in enumerate(same):
        slot += jnp.where(here, counts[g * src_count : (g + 1) * src_count, :], 0.0)
    slot = slot.astype(jnp.int32)
    sent = jnp.where(group == src_index, slot, -1)
    slot_ids = lax.broadcasted_iota(jnp.int32, (capacity, lanes), 0)
    place_ids = lax.broadcasted_iota(jnp.int32, (source_rows, lanes), 0)
    for k in range(src_count):
        from_slot = jnp.where(slot_ids == sent[k : k + 1, :], 1.0, 0.0).astype(bf16)
        from_place = jnp.where(place_ids == place[k : k + 1, :], 1.0, 0.0).astype(bf16)
        pick_out[k * capacity : (k + 1) * capacity, :] = lax.dot_general(
            from_slot, from_place, by_row, preferred_element_type=f32
        ).astype(bf16)
    first_own = recv_index * group_rows + src_index * own_clusters
    code = (target - first_own) * code_base + group * capacity + slot
    own = lax.broadcasted_iota(jnp.int32, code.shape, 0) == src_index
    code = jnp.sum(jnp.where(own, code.astype(f32), 0.0), axis=0, keepdims=True)
    near_out[...] = jnp.transpose(jnp.broadcast_to(code, (lanes, lanes))).astype(jnp.int32)[:tile_count, :]

    per_row = lanes // rank
    group = lanes // per_row
    shape = (group, lanes)
    lane = lax.broadcasted_iota(jnp.int32, shape, 1)
    pick = lax.broadcasted_iota(jnp.int32, shape, 0) * per_row + lane // rank

    def spread(row):
        return jnp.take_along_axis(jnp.broadcast_to(row, shape), pick, axis=1)

    for a in range(rank_ref.shape[0]):
        across = slice(a * lanes, (a + 1) * lanes)
        target = (far_pairs[0:1, across] - recv_index * group_rows) * code_base
        source = spread(target + group_place(far_pairs[1:2, across]))
        missing = spread(target + (code_base - 1))
        far_out[a * group : (a + 1) * group, :] = jnp.where(
            lane % rank < spread(rank_ref[a : a + 1, :]), source, missing
        )
    order = order_ref[...]
    q, a, b, slip = gather_rows([buf[k] for k in range(4)], order // lanes, order % lanes)
    p, plate = mine_ref[0], mine_ref[1]
    speed = jnp.exp(p)
    theta_rate = jnp.exp(-q) - speed / slip
    gain = 1.0 / (a + damping * speed)
    for k, value in enumerate((p, q, a, b, slip, plate, theta_rate, gain)):
        own_out[k] = value
    for copy in heads:
        copy.wait()


def far_part(code_ref, deficit, v_head, u_head, v_buf, u_buf, out_ref, before):
    part = v_buf.shape[0] // chunks
    source_count = deficit.shape[0]
    target_count = out_ref.shape[0]
    source_ids = lax.broadcasted_iota(jnp.int32, (source_count, lanes), 0)
    target_ids = [
        (lax.broadcasted_iota(jnp.int32, (16, lanes), 0) + 16 * k).astype(f32).astype(bf16)
        for k in range(target_count // 16)
    ]
    out_ref[...] = jnp.zeros_like(out_ref)

    step = 0
    for body in bodies:
        base, count = step * part, body * part
        v_ref, u_ref = (v_buf, u_buf) if step else (v_head, u_head)
        if step:
            for i in range(step, step + body):
                before(i)
        products = lax.dot_general(
            deficit, v_ref[base : base + count, :], by_row, preferred_element_type=f32
        )
        spread = []
        for k in range(count // lanes):
            row = base // lanes + k
            code = code_ref[row : row + 1, :]
            source = code % code_base
            target = jnp.broadcast_to((code // code_base).astype(f32), (16, lanes)).astype(bf16)
            coef = jnp.sum(
                jnp.where(source_ids == source, products[:, k * lanes : (k + 1) * lanes], 0.0),
                axis=0,
                keepdims=True,
            )
            coef = jnp.broadcast_to(coef, (16, lanes)).astype(bf16)
            spread.append(
                jnp.concatenate(
                    [jnp.where(ids == target, coef, jnp.zeros_like(coef)) for ids in target_ids], 0
                )
            )
        out_ref[...] += jnp.dot(
            jnp.concatenate(spread, 1), u_ref[base : base + count, :], preferred_element_type=f32
        )
        step += body


def far_kernel(code_ref, pick_ref, *refs):
    parts, (v_head, u_head, v_hbm, u_hbm, out_ref, v_buf, u_buf, sems, total_ref) = refs[:-9], refs[-9:]
    part = v_hbm.shape[0] // chunks

    def copies(i):
        where = slice(i * part, (i + 1) * part)
        return (
            pltpu.make_async_copy(v_hbm.at[where], v_buf.at[where], sems.at[0, i]),
            pltpu.make_async_copy(u_hbm.at[where], u_buf.at[where], sems.at[1, i]),
        )

    for i in range(bodies[0], chunks):
        for copy in copies(i):
            copy.start()

    def before(i):
        for copy in copies(i):
            copy.wait()

    deficit = jnp.concatenate([ref[...] for ref in parts], 0)
    count = parts[0].shape[0]
    picked = jnp.dot(pick_ref[...], deficit, preferred_element_type=f32).astype(bf16)
    capacity = out_ref.shape[1] - count
    for k in range(out_ref.shape[0]):
        out_ref[k, count:, :] = picked[k * capacity : (k + 1) * capacity, :]
    far_part(code_ref, deficit, v_head, u_head, v_buf, u_buf, total_ref, before)
    for k in range(out_ref.shape[0]):
        out_ref[k, :count, :] = total_ref[k * count : (k + 1) * count, :].astype(bf16)


def whole_stress(code_ref, came_ref, tile_ref, count):
    senders = came_ref.shape[0]
    columns = jnp.concatenate([came_ref[k, count:, :] for k in range(senders)], 0)
    tile_count = tile_ref.shape[0]
    code = code_ref[...]
    place, target = code % code_base, code // code_base
    place_ids = lax.broadcasted_iota(jnp.int32, (tile_count, lanes), 1)
    deficits = jnp.zeros((tile_count, lanes), f32)
    for k in range(columns.shape[0] // lanes):
        hot = jnp.where(place_ids + k * lanes == place, 1.0, 0.0).astype(bf16)
        deficits += jnp.dot(hot, columns[k * lanes : (k + 1) * lanes, :], preferred_element_type=f32)
    ids = lax.broadcasted_iota(jnp.int32, (count, lanes), 0)
    placed = [
        jnp.where(ids == target[t : t + 1, :], deficits[t : t + 1, :], 0.0).astype(bf16)
        for t in range(tile_count)
    ]
    near = lax.dot_general(
        jnp.concatenate(placed, 1),
        jnp.concatenate([tile_ref[t] for t in range(tile_count)], 1),
        by_row,
        preferred_element_type=f32,
    )
    far = came_ref[0, :count, :].astype(f32)
    for k in range(1, senders):
        far += came_ref[k, :count, :].astype(f32)
    return far + near


def first_kernel(code_ref, came_ref, tile_ref, own_ref, stress_ref, deficit_ref):
    stress = whole_stress(code_ref, came_ref, tile_ref, stress_ref.shape[0])
    stress_ref[...] = stress
    p, b, plate, theta_rate, gain = [own_ref[k] for k in (0, 3, 5, 6, 7)]
    speed = jnp.exp(p + time_step * ((stress - b * theta_rate) * gain))
    deficit_ref[...] = (plate - speed).astype(bf16)


def ahead_kernel(own_ref, first_ref, order_ref, v_hbm, u_hbm, keep_ref, back_ref, q_out, v_out, u_out, head_sems):
    heads = head_copies(v_hbm, u_hbm, v_out, u_out, head_sems)
    order = order_ref[...]
    rows = order.shape[0]
    row, lane = order // lanes, order % lanes
    row_ids = lax.broadcasted_iota(jnp.int32, (rows, lanes), 0)
    position = lax.broadcasted_iota(jnp.int32, (rows, lanes), 1).astype(f32)
    lane_ids = lax.broadcasted_iota(jnp.int32, (lanes, lanes), 0)
    placed, spread = [], []
    for r in range(rows):
        here = row_ids == row[r : r + 1, :]
        placed.append(jnp.concatenate([jnp.where(here, float(r), 0.0), jnp.where(here, position, 0.0)], 0).astype(bf16))
        spread.append(jnp.where(lane_ids == lane[r : r + 1, :], 1.0, 0.0).astype(bf16))
    total = lax.dot_general(
        jnp.concatenate(placed, 1), jnp.concatenate(spread, 1), by_row, preferred_element_type=f32
    )
    back_row, back_lane = total[:rows].astype(jnp.int32), total[rows:].astype(jnp.int32)
    back_ref[0] = back_row
    back_ref[1] = back_lane

    p, q, a, b, slip, plate, theta_rate, gain = [own_ref[k] for k in range(8)]
    first_p = (first_ref[...] - b * theta_rate) * gain
    speed = jnp.exp(p + time_step * first_p)
    second_q = jnp.exp(-(q + time_step * theta_rate)) - speed / slip
    second_gain = 0.5 * time_step / (a + damping * speed)
    new_q, offset, factor = gather_rows(
        (
            q + 0.5 * time_step * (theta_rate + second_q),
            p + 0.5 * time_step * first_p - b * second_q * second_gain,
            second_gain,
        ),
        back_row,
        back_lane,
    )
    q_out[...] = new_q
    keep_ref[0] = offset
    keep_ref[1] = factor
    for copy in heads:
        copy.wait()


def final_kernel(code_ref, came_ref, tile_ref, keep_ref, back_ref, p_out):
    stress = whole_stress(code_ref, came_ref, tile_ref, p_out.shape[0])
    (stress,) = gather_rows((stress,), back_ref[0], back_ref[1])
    p_out[...] = keep_ref[0] + keep_ref[1] * stress


def on_device(
    log_rate,
    log_state,
    a_sigma,
    b_sigma,
    crit_slip,
    plate_rate,
    cluster_order,
    near_tiles,
    near_pairs,
    far_u,
    far_v,
    far_pairs,
    far_ranks,
):
    src_count = lax.axis_size("src")
    recv_count = lax.axis_size("recv")
    device_count = src_count * recv_count
    tile_count = near_tiles.shape[0]
    own_clusters = log_rate.shape[0] // lanes
    group_rows = own_clusters * src_count
    source_rows = own_clusters * recv_count
    far_count, rank = far_u.shape[:2]
    factor_rows = far_count * rank
    params = pltpu.CompilerParams(vmem_limit_bytes=vmem_bytes)
    whole = (own_clusters, lanes)

    arguments = [x.reshape(whole) for x in (log_rate, log_state, a_sigma, b_sigma, crit_slip, plate_rate)]
    p_hbm, q_hbm, a_hbm, b_hbm, slip_hbm, plate_hbm = [in_hbm(x) for x in arguments]
    mine, first_deficit, order = pl.pallas_call(
        order_kernel,
        in_specs=[anywhere] * 3,
        out_specs=(in_vmem,) * 3,
        out_shape=(
            jax.ShapeDtypeStruct((2,) + whole, f32),
            jax.ShapeDtypeStruct(whole, bf16),
            jax.ShapeDtypeStruct(whole, jnp.int32),
        ),
        scratch_shapes=[pltpu.VMEM((2,) + whole, f32), pltpu.SemaphoreType.DMA((3,))],
        compiler_params=params,
    )(p_hbm, plate_hbm, in_hbm(cluster_order.reshape(whole)))

    v_rows = in_hbm(far_v.reshape(factor_rows, lanes))
    u_rows = in_hbm(far_u.reshape(factor_rows, lanes))
    head = jax.ShapeDtypeStruct((factor_rows // chunks * bodies[0], lanes), bf16)
    capacity = -(-max(2, 2 * tile_count // src_count) // 16) * 16
    far_codes, near_codes, picks, own, *first_heads = pl.pallas_call(
        functools.partial(
            table_kernel, rank=rank, own_clusters=own_clusters, src_count=src_count, capacity=capacity
        ),
        in_specs=[anywhere] * 9 + [in_vmem] * 2,
        out_specs=(in_vmem,) * 6,
        out_shape=(
            jax.ShapeDtypeStruct((factor_rows // lanes, lanes), jnp.int32),
            jax.ShapeDtypeStruct((tile_count, lanes), jnp.int32),
            jax.ShapeDtypeStruct((src_count * capacity, source_rows), bf16),
            jax.ShapeDtypeStruct((8,) + whole, f32),
            head,
            head,
        ),
        scratch_shapes=[
            pltpu.VMEM(near_pairs.shape, jnp.int32),
            pltpu.VMEM(far_pairs.shape, jnp.int32),
            pltpu.VMEM((far_count // lanes, lanes), jnp.int32),
            pltpu.VMEM((4,) + whole, f32),
            pltpu.SemaphoreType.DMA((7,)),
            pltpu.SemaphoreType.DMA((2,)),
        ],
        compiler_params=params,
    )(*[in_hbm(x) for x in (near_pairs, far_pairs, far_ranks.reshape(far_count // lanes, lanes))], q_hbm, a_hbm, b_hbm, slip_hbm, v_rows, u_rows, mine, order)

    def exchange(deficit, heads):
        parts = [deficit] + [
            lax.ppermute(deficit, "recv", [(i, i ^ k) for i in range(recv_count)])
            for k in range(1, recv_count)
        ]
        send = pl.pallas_call(
            far_kernel,
            in_specs=[in_vmem] * (4 + recv_count) + [anywhere] * 2,
            out_specs=in_vmem,
            out_shape=jax.ShapeDtypeStruct((src_count, own_clusters + capacity, lanes), bf16),
            scratch_shapes=[
                pltpu.VMEM(v_rows.shape, bf16),
                pltpu.VMEM(u_rows.shape, bf16),
                pltpu.SemaphoreType.DMA((2, chunks)),
                pltpu.VMEM((group_rows, lanes), f32),
            ],
            compiler_params=pltpu.CompilerParams(vmem_limit_bytes=far_vmem_bytes),
            cost_estimate=pl.CostEstimate(
                flops=2 * factor_rows * lanes * (source_rows + group_rows), bytes_accessed=2**24, transcendentals=0
            ),
        )(far_codes, picks, *parts, *heads, v_rows, u_rows)
        return lax.all_to_all(send, "src", split_axis=0, concat_axis=0, tiled=True)

    state = jax.ShapeDtypeStruct(whole, f32)
    first_stress, second_deficit = pl.pallas_call(
        first_kernel,
        in_specs=[in_vmem] * 4,
        out_specs=(in_vmem,) * 2,
        out_shape=(state, jax.ShapeDtypeStruct(whole, bf16)),
        compiler_params=params,
    )(near_codes, exchange(first_deficit, first_heads), near_tiles, own)
    keep, back, new_q, *second_heads = pl.pallas_call(
        ahead_kernel,
        in_specs=[in_vmem] * 3 + [anywhere] * 2,
        out_specs=(in_vmem,) * 5,
        out_shape=(
            jax.ShapeDtypeStruct((2,) + whole, f32),
            jax.ShapeDtypeStruct((2,) + whole, jnp.int32),
            state,
            head,
            head,
        ),
        scratch_shapes=[pltpu.SemaphoreType.DMA((2,))],
        compiler_params=params,
    )(own, first_stress, order, v_rows, u_rows)
    new_p = pl.pallas_call(
        final_kernel,
        in_specs=[in_vmem] * 5,
        out_specs=in_vmem,
        out_shape=state,
        compiler_params=params,
    )(near_codes, exchange(second_deficit, second_heads), near_tiles, keep, back)
    return new_p.reshape(-1), new_q.reshape(-1)


def solution(mesh):
    return jax.shard_map(
        on_device,
        mesh=mesh,
        in_specs=(
            P(("recv", "src")),
            P(("recv", "src")),
            P(("recv", "src")),
            P(("recv", "src")),
            P(("recv", "src")),
            P(("recv", "src")),
            P(("recv", "src"), None),
            P(("recv", "src"), None, None),
            P(None, "recv"),
            P(("recv", "src"), None, None),
            P(("recv", "src"), None, None),
            P(None, ("recv", "src")),
            P(("recv", "src")),
        ),
        out_specs=(P(("recv", "src")), P(("recv", "src"))),
        check_vma=False,
    )
```
